32 devices in a mesh: dp: 8 (over z, x), seq: 4 (over y, core).
Axes of the slice: x: 2, y: 2, z: 4, core: 2. Of those that a mesh axis runs over, the one named last changes fastest.
Arguments:
- canvas: bfloat16 [2, 8, 1024, 512], P(None, 'dp', 'seq'), may hold values from -6 to 6
- memory: bfloat16 [2, 8, 1024, 512], P(None, 'dp', 'seq'), may hold values from -6 to 6
- canvas_len: int32 [2, 8], P(None, 'dp'), may hold values from 512 to 1024, as said below
- memory_len: int32 [2, 8], P(None, 'dp'), may hold values from 512 to 1024, as said below
- slot_cot: bfloat16 [2, 8, 1024, 512], P(None, 'dp', 'seq'), may hold values from -6 to 6
- self_project: bfloat16 [3, 512, 512], replicated, may hold values from -0.25 to 0.25
- self_output: bfloat16 [512, 512], replicated, may hold values from -4 to 4
- self_biases: bfloat16 [3, 512], replicated, may hold values from -3 to 3
- cross_project: bfloat16 [3, 512, 512], replicated, may hold values from -0.25 to 0.25
- cross_output: bfloat16 [512, 512], replicated, may hold values from -4 to 4
- cross_biases: bfloat16 [3, 512], replicated, may hold values from -3 to 3
- norm_gains: bfloat16 [3, 512], replicated, may hold values from 0.25 to 1.75
- norm_shifts: bfloat16 [3, 512], replicated, may hold values from -3 to 3
- inner_weight: bfloat16 [512, 2048], replicated, may hold values from -0.25 to 0.25
- inner_bias: bfloat16 [2048], replicated, may hold values from -3 to 3
- outer_weight: bfloat16 [2048, 512], replicated, may hold values from -0.125 to 0.125
- outer_bias: bfloat16 [512], replicated, may hold values from -3 to 3
- slot_weight: bfloat16 [1024, 512], replicated, may hold values from -0.1875 to 0.1875
- slot_bias: bfloat16 [512], replicated, may hold values from -3 to 3
Outputs:
- slot_states: bfloat16 [2, 8, 1024, 512], P(None, 'dp', 'seq')
- canvas_grad: float32 [2, 8, 1024, 512], P(None, 'dp', 'seq')
- memory_grad: float32 [2, 8, 1024, 512], P(None, 'dp', 'seq')
- grad_self_project: float32 [3, 512, 512], replicated
- grad_self_output: float32 [512, 512], replicated
- grad_self_biases: float32 [3, 512], replicated
- grad_cross_project: float32 [3, 512, 512], replicated
- grad_cross_output: float32 [512, 512], replicated
- grad_cross_biases: float32 [3, 512], replicated
- grad_norm_gains: float32 [3, 512], replicated
- grad_norm_shifts: float32 [3, 512], replicated
- grad_inner_weight: float32 [512, 2048], replicated
- grad_inner_bias: float32 [2048], replicated
- grad_outer_weight: float32 [2048, 512], replicated
- grad_outer_bias: float32 [512], replicated
- grad_slot_weight: float32 [1024, 512], replicated
- grad_slot_bias: float32 [512], replicated
The draws below stay inside these ranges and needn't reach their ends.
Inputs may be any that keep to these rules, and one draw needn't show every extreme that they name: `canvas_len`: in every canvas column b, the canvas of one micro-batch, drawn from the seed, has exactly 1024 live positions. `memory_len`: in every canvas column b, the memory of one micro-batch, drawn from the seed, has exactly 1024 live positions.
All inputs are finite; a program needn't handle non-finite values.
Results may differ from the reference program's by a relative error of at most 0.024.
Values may be sent and summed in bfloat16 or wider, within the bound.
No kernel may reach another device: no remote copies, remote signals or barrier semaphores. Data moves between devices by JAX's collectives and lax.ppermute only.
A program may use at most 192 MiB of HBM per device.

```python
import jax
import jax.numpy as jnp
from jax import lax

D = 512
HEADS = 8
FF = 2048
MB = 2
M = 1024
L = 1024
BATCH = 8


def ragged(key, low_end, high_end):
    first, second = jax.random.split(key)
    base = jax.random.randint(first, (MB, BATCH), low_end, high_end + 1)
    chosen = jax.random.randint(second, (BATCH,), 0, MB)
    marked = jnp.arange(MB)[:, None] == chosen[None, :]
    return jnp.where(marked, high_end, base).astype(jnp.int32)


def draw_canvas_len(key, part):
    key = jax.random.fold_in(key, 11)
    return ragged(key, L // 2, L)


def draw_memory_len(key, part):
    key = jax.random.fold_in(key, 23)
    return ragged(key, M // 2, M)


def level_of(rng, dims, cuts, low, top_value):
    factor_of, own = 1.0, jax.random.fold_in(rng, 6)
    for axis_at, blocks in cuts:
        heights = jnp.exp(jax.random.uniform(jax.random.fold_in(own, axis_at), (blocks,), jnp.float32, low / len(cuts), top_value / len(cuts)))
        factor_of = factor_of * jnp.repeat(heights, dims[axis_at] // blocks).reshape([-1 if axis == axis_at else 1 for axis in range(len(dims))])
    return factor_of


def bell_draw(rng, extent, scale, reach, cuts=(), kind=jnp.bfloat16):
    array = scale * jax.random.normal(rng, extent, jnp.float32)
    if cuts:
        array = array * level_of(rng, extent, cuts, -0.22, 0.18)
    return jnp.clip(array, -reach, reach).astype(kind)


def setup_inputs(seed: int = 0) -> dict:
    arg_keys = jax.random.split(jax.random.key(seed), 20)
    return {
        "canvas": bell_draw(arg_keys[0], (MB, BATCH, L, D), 1.0, 6.0, ((1, 8), (2, 4))),
        "memory": bell_draw(arg_keys[1], (MB, BATCH, M, D), 1.0, 6.0, ((1, 8), (2, 4))),
        "canvas_len": draw_canvas_len(jax.random.fold_in(arg_keys[19], 71), 0),
        "memory_len": draw_memory_len(jax.random.fold_in(arg_keys[19], 71), 0),
        "slot_cot": bell_draw(arg_keys[4], (MB, BATCH, L, D), 1.0, 6.0, ((1, 8), (2, 4))),
        "self_project": bell_draw(arg_keys[5], (3, D, D), D ** -0.5, 0.25),
        "self_output": bell_draw(arg_keys[6], (D, D), (max(D // 256, 1)) ** -0.5, 4.0),
        "self_biases": bell_draw(arg_keys[7], (3, D), 0.5, 3.0),
        "cross_project": bell_draw(arg_keys[8], (3, D, D), D ** -0.5, 0.25),
        "cross_output": bell_draw(arg_keys[9], (D, D), (max(D // 256, 1)) ** -0.5, 4.0),
        "cross_biases": bell_draw(arg_keys[10], (3, D), 0.5, 3.0),
        "norm_gains": jnp.clip(1.0 + 0.15 * jax.random.normal(arg_keys[11], (3, D), jnp.float32), 0.25, 1.75).astype(jnp.bfloat16),
        "norm_shifts": bell_draw(arg_keys[12], (3, D), 0.5, 3.0),
        "inner_weight": bell_draw(arg_keys[13], (D, FF), D ** -0.5, 0.25),
        "inner_bias": bell_draw(arg_keys[14], (FF,), 0.5, 3.0),
        "outer_weight": bell_draw(arg_keys[15], (FF, D), FF ** -0.5, 0.125),
        "outer_bias": bell_draw(arg_keys[16], (D,), 0.5, 3.0),
        "slot_weight": bell_draw(arg_keys[17], (2 * D, D), (2 * D) ** -0.5, 0.1875),
        "slot_bias": bell_draw(arg_keys[18], (D,), 0.5, 3.0),
    }


epsilon = 1e-05
exact = lax.Precision.HIGHEST

@jax.custom_vjp
def low(v):
    return lax.optimization_barrier(v.astype(jnp.bfloat16)).astype(jnp.float32)

@jax.custom_vjp
def low_back(v):
    return v

def low_keep(v):
    return (low(v), None)

def low_pass(kept, grad):
    return (grad,)

def back_keep(v):
    return (v, None)

def back_low(kept, grad):
    return (low(grad),)
low.defvjp(low_keep, low_pass)
low_back.defvjp(back_keep, back_low)

def product(left, right):
    return jnp.dot(left, right, precision=exact, preferred_element_type=jnp.float32)

def norm(value, gain, shift):
    mean = lax.optimization_barrier(jnp.mean(value, -1, keepdims=True))
    centered = value - mean
    spread = lax.optimization_barrier(jnp.mean(centered * centered, -1, keepdims=True))
    return centered * lax.rsqrt(spread + epsilon) * gain + shift

def attention(query, keys, values, allowed):
    rows = query.shape[0]
    block = min(512, rows)
    count = rows // block
    head_dim = query.shape[1] // HEADS
    scale = head_dim ** (-0.5)
    key_heads = keys.reshape(keys.shape[0], HEADS, head_dim)
    value_heads = values.reshape(values.shape[0], HEADS, head_dim)

    def one_block(piece):
        heads = piece.reshape(block, HEADS, head_dim)
        scores = jnp.einsum('rhd,khd->hrk', heads, key_heads, precision=exact) * scale
        scores = low_back(scores)
        scores = jnp.where(allowed[None, None, :], scores, -1e+30)
        weights = low(jax.nn.softmax(scores, axis=-1))
        mixed = jnp.einsum('hrk,khd->rhd', weights, value_heads, precision=exact)
        return mixed.reshape(block, HEADS * head_dim)
    result = lax.map(jax.checkpoint(one_block), query.reshape(count, block, query.shape[1]))
    return result.reshape(rows, query.shape[1])

def layer(tokens, source, params, allowed, mem_allowed, live):
    self_project, self_output, self_biases, cross_project, cross_output, cross_biases, norm_gains, norm_shifts, inner_weight, inner_bias, outer_weight, outer_bias, slot_weight, slot_bias = params
    query = low(low_back(product(tokens, self_project[0])) + self_biases[0])
    keys = low(low_back(product(tokens, self_project[1])))
    values = low(low_back(product(tokens, self_project[2])) + self_biases[1])
    mixed = low(low_back(attention(query, keys, values, allowed)))
    first = tokens + low_back(product(mixed, self_output)) + self_biases[2]
    normed_one = norm(first, norm_gains[0], norm_shifts[0])
    normed_low = low(normed_one)
    query_two = low(low_back(product(normed_low, cross_project[0])) + cross_biases[0])
    keys_two = low(low_back(product(source, cross_project[1])))
    values_two = low(low_back(product(source, cross_project[2])) + cross_biases[1])
    cross_mixed = low(low_back(attention(query_two, keys_two, values_two, mem_allowed)))
    second = normed_one + low_back(product(cross_mixed, cross_output)) + cross_biases[2]
    normed_two = norm(second, norm_gains[1], norm_shifts[1])
    inner = low_back(product(low(normed_two), inner_weight)) + inner_bias
    active = low(jax.nn.gelu(inner, approximate=True))
    third = normed_two + low_back(product(active, outer_weight)) + outer_bias
    state = low(norm(third, norm_gains[2], norm_shifts[2]))
    following = jnp.concatenate([state[1:], jnp.zeros((1, state.shape[1]), jnp.float32)], 0)
    joined = jnp.concatenate([state, following], 1)
    slots = product(joined, slot_weight) + slot_bias
    return jnp.where(live[:, None], slots, 0.0)

def reference(canvas, memory, canvas_len, memory_len, slot_cot, self_project, self_output, self_biases, cross_project, cross_output, cross_biases, norm_gains, norm_shifts, inner_weight, inner_bias, outer_weight, outer_bias, slot_weight, slot_bias):
    params = tuple((item.astype(jnp.float32) for item in (self_project, self_output, self_biases, cross_project, cross_output, cross_biases, norm_gains, norm_shifts, inner_weight, inner_bias, outer_weight, outer_bias, slot_weight, slot_bias)))
    count = MB * BATCH
    inputs = (canvas.astype(jnp.float32).reshape(count, L, D), memory.astype(jnp.float32).reshape(count, M, D), slot_cot.astype(jnp.float32).reshape(count, L, D), canvas_len.reshape(count).astype(jnp.int32), memory_len.reshape(count).astype(jnp.int32))
    positions = jnp.arange(L, dtype=jnp.int32)
    mem_positions = jnp.arange(M, dtype=jnp.int32)

    def advance(totals, item):
        tokens, source, cotangent, canvas_size, memory_size = item
        allowed = positions < canvas_size
        mem_allowed = mem_positions < memory_size
        live = positions + 1 < canvas_size

        def forward(tokens_in, source_in, weights):
            return layer(tokens_in, source_in, weights, allowed, mem_allowed, live)
        slots, pull = jax.vjp(forward, tokens, source, params)
        tokens_grad, source_grad, weight_grads = pull(cotangent)
        totals = jax.tree.map(lambda left, right: left + right, totals, weight_grads)
        return (totals, (slots.astype(jnp.bfloat16), tokens_grad, source_grad))
    zeros = tuple((jnp.zeros_like(item) for item in params))
    totals, (slots, tokens_grad, source_grad) = lax.scan(advance, zeros, inputs)
    return (slots.reshape(MB, BATCH, L, D), tokens_grad.reshape(MB, BATCH, L, D), source_grad.reshape(MB, BATCH, M, D), totals[0], totals[1], totals[2], totals[3], totals[4], totals[5], totals[6], totals[7], totals[8], totals[9], totals[10], totals[11], totals[12], totals[13])
```

```python
import functools

import jax
import jax.numpy as jnp
from jax import lax
from jax.experimental import pallas as pl
from jax.experimental.pallas import tpu as pltpu
from jax.sharding import PartitionSpec as P

LANES = 128
CHUNK = 256
EPSILON = 1e-05
MASKED = -1e30
F32 = jnp.float32
BF16 = jnp.bfloat16
BLOCKS = (0, 2, 1, 3)


def product(left, right):
    return jnp.dot(left, right, preferred_element_type=F32)


def left_product(left, right):
    return lax.dot_general(left, right, (((0,), (0,)), ((), ())), preferred_element_type=F32)


def right_product(left, right):
    return lax.dot_general(left, right, (((1,), (1,)), ((), ())), preferred_element_type=F32)


def column_sum(value):
    return jnp.sum(value, 0, keepdims=True)


def norm_forward(value):
    mean = jnp.mean(value, -1, keepdims=True)
    centered = value - mean
    spread = jnp.mean(centered * centered, -1, keepdims=True)
    inverse = lax.rsqrt(spread + EPSILON)
    return centered * inverse, inverse


def norm_backward(upstream, normal, inverse, gain):
    scaled = upstream * gain
    inner_mean = jnp.mean(scaled, -1, keepdims=True)
    cross_mean = jnp.mean(scaled * normal, -1, keepdims=True)
    return inverse * (scaled - inner_mean - normal * cross_mean)


def wide_row(ref, row):
    return ref[row : row + 1, :].astype(F32)


def head_only(value, which):
    lane = lax.broadcasted_iota(jnp.int32, (1, LANES), 1)
    mine = lane < LANES // 2 if which == 0 else lane >= LANES // 2
    return jnp.where(mine, value, jnp.zeros_like(value))


def head_pick(first, second):
    lane = lax.broadcasted_iota(jnp.int32, (1, LANES), 1)
    return jnp.where(lane < LANES // 2, first, second)


def pair_of(step):
    return pl.ds(pl.multiple_of(step * LANES, LANES), LANES)


def forward_body(cross, scalars, rows_in, all_in, wq, wk, wv, biases, wo, gains, shifts, *refs):
    if cross:
        out_low, *refs = refs
    out_q, out_k, out_v, out_p, out_o, out_inverse, out_normal, out_spread = refs
    step = pl.program_id(0)
    rows = rows_in.shape[0]
    total = all_in.shape[0]
    block = total // len(BLOCKS)
    seat, size = scalars[0], scalars[2 if cross else 1]

    if cross:

        @pl.when(step == 0)
        def _():
            value = rows_in[...] * wide_row(gains, 0) + wide_row(shifts, 0)
            out_low[...] = value.astype(BF16)

        source = out_low
    else:
        source = rows_in

    query = product(source[...], wq[0]) + biases[0:1, pair_of(step)].astype(F32)
    query = query.astype(BF16) * jnp.asarray(0.125, BF16)
    out_q[...] = query
    both = product(all_in[...], jnp.concatenate([wk[0], wv[0]], 1))
    keys = both[:, :LANES].astype(BF16)
    values = (both[:, LANES:] + biases[1:2, pair_of(step)].astype(F32)).astype(BF16)
    out_k[...] = keys
    out_v[...] = values
    wide = jnp.concatenate([values, jnp.ones((total, LANES), BF16)], 1)
    place = lax.broadcasted_iota(jnp.int32, (1, block), 1)
    bias = jnp.concatenate(
        [jnp.where((seat ^ item) * block + place < size, 0.0, MASKED) for item in BLOCKS], 1
    )
    for start in range(0, rows, CHUNK):
        piece = query[start : start + CHUNK]
        parts = []
        for head in range(2):
            scores = right_product(head_only(piece, head), keys) + bias
            weights = jnp.exp(scores - jnp.max(scores, 1, keepdims=True)).astype(BF16)
            out_p[head, start : start + CHUNK, :] = weights
            result = product(weights, wide)
            inverse = 1.0 / result[:, LANES:]
            parts.append((result[:, :LANES] * inverse, inverse))
        out_o[start : start + CHUNK, pair_of(step)] = head_pick(parts[0][0], parts[1][0]).astype(BF16)
        out_inverse[start : start + CHUNK, pair_of(step)] = head_pick(parts[0][1], parts[1][1])

    @pl.when(step == pl.num_programs(0) - 1)
    def _():
        if cross:
            base = rows_in[...] * wide_row(gains, 0) + wide_row(shifts, 0)
        else:
            base = rows_in[...].astype(F32)
        value = base + product(out_o[...], wo[...]) + wide_row(biases, 2)
        normal, inverse = norm_forward(value)
        out_normal[...] = normal
        out_spread[...] = jnp.broadcast_to(inverse, out_spread.shape)


def attention_forward(cross, scalars, rows_in, all_in, project, biases, wo, gains, shifts):
    rows, width = rows_in.shape
    total = all_in.shape[0]
    pairs = width // LANES
    whole = lambda *shape: pl.BlockSpec(shape, lambda i: (0,) * len(shape))
    part = lambda count: pl.BlockSpec((count, LANES), lambda i: (0, i))
    weight = lambda which: pl.BlockSpec((1, width, LANES), lambda i: (which, 0, i))
    out_shape = [
        jax.ShapeDtypeStruct((rows, width), BF16),
        jax.ShapeDtypeStruct((total, width), BF16),
        jax.ShapeDtypeStruct((total, width), BF16),
        jax.ShapeDtypeStruct((2 * pairs, rows, total), BF16),
        jax.ShapeDtypeStruct((rows, width), BF16),
        jax.ShapeDtypeStruct((rows, width), F32),
        jax.ShapeDtypeStruct((rows, width), F32),
        jax.ShapeDtypeStruct((rows, LANES), F32),
    ]
    out_specs = [
        part(rows),
        part(total),
        part(total),
        pl.BlockSpec((2, rows, total), lambda i: (i, 0, 0)),
        whole(rows, width),
        whole(rows, width),
        whole(rows, width),
        whole(rows, LANES),
    ]
    if cross:
        out_shape = [jax.ShapeDtypeStruct((rows, width), BF16)] + out_shape
        out_specs = [whole(rows, width)] + out_specs
    return pl.pallas_call(
        functools.partial(forward_body, cross),
        grid=(pairs,),
        in_specs=[
            pl.BlockSpec(memory_space=pltpu.SMEM),
            whole(rows, width),
            whole(total, width),
            weight(0),
            weight(1),
            weight(2),
            whole(3, width),
            whole(width, width),
            whole(3, width),
            whole(3, width),
        ],
        out_specs=out_specs,
        out_shape=out_shape,
        compiler_params=pltpu.CompilerParams(vmem_limit_bytes=40 << 20),
        cost_estimate=pl.CostEstimate(
            flops=2 * rows * total * width * 8, bytes_accessed=20 << 20, transcendentals=rows * total * 8
        ),
        name="cross_forward" if cross else "self_forward",
    )(scalars, rows_in, all_in, project, project, project, biases, wo, gains, shifts)


def backward_body(cross, scalars, upstream, normal, spread, gains, mixed, inverse, query, keys, values, weights,
                  rows_in, all_in, wq, wk, wv, wo,
                  out_keep, out_send, out_small, out_rows, out_own, out_other, mixed_grad, all_acc):
    step = pl.program_id(0)
    last = pl.num_programs(0) - 1
    rows, width = rows_in.shape
    total = all_in.shape[0]
    even = lax.rem(scalars[0], 2) == 0
    which_norm = 1 if cross else 0

    def store(kept_by_even, index, columns, value):
        @pl.when(even if kept_by_even else jnp.logical_not(even))
        def _():
            out_keep[index, :, columns] = value

        @pl.when(jnp.logical_not(even) if kept_by_even else even)
        def _():
            out_send[index, :, columns] = value

    @pl.when(step == 0)
    def _():
        grad = norm_backward(upstream[...], normal[...], spread[:, 0:1], wide_row(gains, which_norm))
        out_small[...] = jnp.zeros(out_small.shape, F32)
        out_small[0:1, :] = column_sum(upstream[...] * normal[...])
        out_small[1:2, :] = column_sum(upstream[...])
        out_small[2:3, :] = column_sum(grad)
        out_rows[...] = grad
        low = grad.astype(BF16)
        store(True, 0, slice(None), left_product(mixed[...], low).astype(BF16))
        mixed_grad[...] = (right_product(low, wo[...]) * inverse[...]).astype(BF16)

    pair = pair_of(step)
    keys_now, values_now = keys[...], values[...]
    key_grad = jnp.zeros((total, LANES), F32)
    value_grad = jnp.zeros((total, LANES), F32)
    query_grads = []
    for start in range(0, rows, CHUNK):
        span = slice(start, start + CHUNK)
        piece = query[span, :]
        grad = mixed_grad[span, pair]
        center = grad.astype(F32) * mixed[span, pair].astype(F32)
        found = []
        for head in range(2):
            grad_now = head_only(grad, head)
            center_now = jnp.sum(head_only(center, head), 1, keepdims=True)
            weight = weights[head, span, :]
            slope = right_product(grad_now, values_now)
            score_grad = (weight.astype(F32) * (slope - center_now)).astype(BF16)
            found.append(product(score_grad, keys_now))
            value_grad = value_grad + left_product(weight, grad_now)
            key_grad = key_grad + left_product(score_grad, head_only(piece, head))
        query_grads.append(head_pick(found[0], found[1]) * 0.125)
    query_grad = jnp.concatenate(query_grads, 0)
    out_small[3:4, pair] = column_sum(query_grad)
    out_small[4:5, pair] = column_sum(value_grad)
    query_low = query_grad.astype(BF16)
    both = jnp.concatenate([key_grad.astype(BF16), value_grad.astype(BF16)], 1)
    store(True, 1, pair, left_product(rows_in[...], query_low).astype(BF16))
    both_grad = left_product(all_in[...], both).astype(BF16)
    store(False, 0, pair, both_grad[:, :LANES])
    store(False, 1, pair, both_grad[:, LANES:])
    out_rows[...] += right_product(query_low, wq[0])
    spread_out = right_product(both, jnp.concatenate([wk[0], wv[0]], 1))

    @pl.when(step == 0)
    def _():
        all_acc[...] = spread_out

    @pl.when(step > 0)
    def _():
        all_acc[...] += spread_out

    @pl.when(step == last)
    def _():
        if cross:
            out_own[...] = all_acc[:rows, :].astype(BF16)
        else:
            out_rows[...] += all_acc[:rows, :]
            out_own[...] = jnp.zeros(out_own.shape, BF16)
        out_other[...] = all_acc[rows:, :].astype(BF16)


def attention_backward(cross, scalars, upstream, normal, spread, gains, mixed, inverse, query, keys, values, weights,
                       rows_in, all_in, project, wo):
    rows, width = rows_in.shape
    total = all_in.shape[0]
    pairs = width // LANES
    whole = lambda *shape: pl.BlockSpec(shape, lambda i: (0,) * len(shape))
    part = lambda count: pl.BlockSpec((count, LANES), lambda i: (0, i))
    weight = lambda which: pl.BlockSpec((1, width, LANES), lambda i: (which, 0, i))
    return pl.pallas_call(
        functools.partial(backward_body, cross),
        grid=(pairs,),
        in_specs=[
            pl.BlockSpec(memory_space=pltpu.SMEM),
            whole(rows, width),
            whole(rows, width),
            whole(rows, LANES),
            whole(3, width),
            whole(rows, width),
            whole(rows, width),
            part(rows),
            part(total),
            part(total),
            pl.BlockSpec((2, rows, total), lambda i: (i, 0, 0)),
            whole(rows, width),
            whole(total, width),
            weight(0),
            weight(1),
            weight(2),
            whole(width, width),
        ],
        out_specs=[
            whole(2, width, width),
            whole(2, width, width),
            whole(8, width),
            whole(rows, width),
            whole(rows, width),
            whole(total - rows, width),
        ],
        out_shape=[
            jax.ShapeDtypeStruct((2, width, width), BF16),
            jax.ShapeDtypeStruct((2, width, width), BF16),
            jax.ShapeDtypeStruct((8, width), F32),
            jax.ShapeDtypeStruct((rows, width), F32),
            jax.ShapeDtypeStruct((rows, width), BF16),
            jax.ShapeDtypeStruct((total - rows, width), BF16),
        ],
        scratch_shapes=[pltpu.VMEM((rows, width), BF16), pltpu.VMEM((total, width), F32)],
        compiler_params=pltpu.CompilerParams(vmem_limit_bytes=48 << 20),
        cost_estimate=pl.CostEstimate(
            flops=2 * rows * total * width * 16, bytes_accessed=20 << 20, transcendentals=0
        ),
        name="cross_backward" if cross else "self_backward",
    )(scalars, upstream, normal, spread, gains, mixed, inverse, query, keys, values, weights, rows_in, all_in,
      project, project, project, wo)


def gelu_parts(value):
    inner = 0.7978845608028654 * (value + 0.044715 * value * value * value)
    return jnp.tanh(inner)


def feed_body(parts, scalars, normal_two, gains, shifts, cotangent, halo, wi, bi, wo, bo, slot_weight,
              out_keep, out_send, out_state, out_grad, out_small,
              low, hidden, active, acc, low_grad):
    step = pl.program_id(0)
    rows, width = normal_two.shape
    block = rows // 2
    seat, size = scalars[0], scalars[1]
    even = lax.rem(seat, 2) == 0

    def store(kept_by_even, index, value):
        @pl.when(even if kept_by_even else jnp.logical_not(even))
        def _():
            out_keep[index] = value

        @pl.when(jnp.logical_not(even) if kept_by_even else even)
        def _():
            out_send[index] = value

    @pl.when(step == 0)
    def _():
        value = normal_two[...] * wide_row(gains, 1) + wide_row(shifts, 1)
        low[...] = value.astype(BF16)
        acc[...] = value + bo[...].astype(F32)

    @pl.when(step < parts)
    def _():
        value = product(low[...], wi[...]) + bi[...].astype(F32)
        hidden[step] = value
        lowered = (0.5 * value * (1.0 + gelu_parts(value))).astype(BF16)
        active[step] = lowered
        acc[...] += product(lowered, wo[...])

    @pl.when(step == parts)
    def _():
        normal, inverse = norm_forward(acc[...])
        state = (normal * wide_row(gains, 2) + wide_row(shifts, 2)).astype(BF16)
        out_state[...] = state
        out_small[...] = jnp.zeros(out_small.shape, F32)
        place = lax.broadcasted_iota(jnp.int32, (block, 1), 0)
        sides = []
        for index, item in enumerate(BLOCKS[:2]):
            first = (seat ^ item) * block
            value = cotangent[index * block : (index + 1) * block, :].astype(F32)
            straight = jnp.where(first + place + 1 < size, value, 0.0)
            before = jnp.where(even, wide_row(halo, 1 - index), wide_row(halo, index))
            moved = jnp.where(place == 0, before, pltpu.roll(value, 1, 0))
            moved = jnp.where((first + place < size) & (first + place > 0), moved, 0.0)
            sides.append((straight, moved))
        straight = jnp.concatenate([sides[0][0], sides[1][0]], 0)
        moved = jnp.concatenate([sides[0][1], sides[1][1]], 0)
        out_small[0:1, :] = column_sum(straight)
        straight, moved = straight.astype(BF16), moved.astype(BF16)
        store(True, 0, left_product(state, straight).astype(BF16))
        store(False, 0, left_product(state, moved).astype(BF16))
        state_grad = right_product(straight, slot_weight[:width, :]) + right_product(moved, slot_weight[width:, :])
        out_small[1:2, :] = column_sum(state_grad * normal)
        out_small[2:3, :] = column_sum(state_grad)
        grad = norm_backward(state_grad, normal, inverse, wide_row(gains, 2))
        out_small[3:4, :] = column_sum(grad)
        acc[...] = grad
        low_grad[...] = grad.astype(BF16)

    @pl.when(step > parts)
    def _():
        index = step - parts - 1
        upstream = right_product(low_grad[...], wo[...])
        value = hidden[index]
        bent = gelu_parts(value)
        slope = 0.5 * (1.0 + bent) + 0.5 * value * (1.0 - bent * bent) * (
            0.7978845608028654 * (1.0 + 3 * 0.044715 * value * value)
        )
        grad = upstream * slope
        out_small[pl.ds(4 + index, 1), :] = column_sum(grad)
        grad_low = grad.astype(BF16)
        store(True, 0, left_product(active[index], low_grad[...]).astype(BF16))
        store(False, 0, left_product(low[...], grad_low).astype(BF16))
        acc[...] += right_product(grad_low, wi[...])

    @pl.when(step == pl.num_programs(0) - 1)
    def _():
        out_grad[...] = acc[...]


def feed_forward(scalars, normal_two, gains, shifts, cotangent, halo, wi, bi, wo, bo, slot_weight):
    rows, width = normal_two.shape
    parts = wi.shape[1] // width
    whole = lambda *shape: pl.BlockSpec(shape, lambda i: (0,) * len(shape))
    part = lambda i: jnp.where(i < parts, i, jnp.maximum(i - parts - 1, 0))
    group = pl.BlockSpec((1, width, width), lambda i: (jnp.maximum(i - parts, 0), 0, 0))
    return pl.pallas_call(
        functools.partial(feed_body, parts),
        grid=(2 * parts + 1,),
        in_specs=[
            pl.BlockSpec(memory_space=pltpu.SMEM),
            whole(rows, width),
            whole(3, width),
            whole(3, width),
            whole(rows, width),
            whole(2, width),
            pl.BlockSpec((width, width), lambda i: (0, part(i))),
            pl.BlockSpec((1, width), lambda i: (0, part(i))),
            pl.BlockSpec((width, width), lambda i: (part(i), 0)),
            whole(1, width),
            whole(2 * width, width),
        ],
        out_specs=[group, group, whole(rows, width), whole(rows, width), whole(8, width)],
        out_shape=[
            jax.ShapeDtypeStruct((parts + 1, width, width), BF16),
            jax.ShapeDtypeStruct((parts + 1, width, width), BF16),
            jax.ShapeDtypeStruct((rows, width), BF16),
            jax.ShapeDtypeStruct((rows, width), F32),
            jax.ShapeDtypeStruct((8, width), F32),
        ],
        scratch_shapes=[
            pltpu.VMEM((rows, width), BF16),
            pltpu.VMEM((parts, rows, width), F32),
            pltpu.VMEM((parts, rows, width), BF16),
            pltpu.VMEM((rows, width), F32),
            pltpu.VMEM((rows, width), BF16),
        ],
        compiler_params=pltpu.CompilerParams(vmem_limit_bytes=40 << 20),
        cost_estimate=pl.CostEstimate(
            flops=2 * rows * width * width * 32, bytes_accessed=20 << 20, transcendentals=rows * width * 8
        ),
        name="feed_forward",
    )(scalars, normal_two, gains, shifts, cotangent, halo, wi, bi.reshape(1, -1), wo, bo.reshape(1, -1), slot_weight)


def slot_body(scalars, state, halo, slot_weight, slot_bias, out):
    rows, width = state.shape
    block = rows // 2
    seat, size = scalars[0], scalars[1]
    even = lax.rem(seat, 2) == 0
    place = lax.broadcasted_iota(jnp.int32, (block, 1), 0)
    for index, item in enumerate(BLOCKS[:2]):
        span = slice(index * block, (index + 1) * block)
        value = state[span, :]
        after = jnp.where(even, wide_row(halo, index), wide_row(halo, 1 - index))
        moved = jnp.where(place == block - 1, after, pltpu.roll(value.astype(F32), block - 1, 0)).astype(BF16)
        result = product(value, slot_weight[:width, :]) + product(moved, slot_weight[width:, :])
        result = result + slot_bias[...].astype(F32)
        out[span, :] = jnp.where((seat ^ item) * block + place + 1 < size, result, 0.0).astype(BF16)


def slot_states(scalars, state, halo, slot_weight, slot_bias):
    rows, width = state.shape
    vmem = pl.BlockSpec(memory_space=pltpu.VMEM)
    return pl.pallas_call(
        slot_body,
        in_specs=[pl.BlockSpec(memory_space=pltpu.SMEM)] + [vmem] * 4,
        out_specs=vmem,
        out_shape=jax.ShapeDtypeStruct((rows, width), BF16),
        compiler_params=pltpu.CompilerParams(vmem_limit_bytes=16 << 20),
        cost_estimate=pl.CostEstimate(flops=4 * rows * width * width, bytes_accessed=4 << 20, transcendentals=0),
        name="slot_states",
    )(scalars, state, halo, slot_weight, slot_bias.reshape(1, -1))


def swap(value, axis, bit):
    count = lax.axis_size(axis)
    return lax.ppermute(value, axis, [(place, place ^ bit) for place in range(count)])


def bit_of(axis, bit):
    return (lax.axis_index(axis) // bit) % 2


def halving(value, route):
    for axis, bit in route:
        half = value.shape[0] // 2
        mine = bit_of(axis, bit) * half
        kept = lax.dynamic_slice_in_dim(value, mine, half, 0)
        sent = lax.dynamic_slice_in_dim(value, half - mine, half, 0)
        value = kept + swap(sent, axis, bit)
    return value


def doubling(value, route):
    for axis, bit in reversed(route):
        got = swap(value, axis, bit)
        lower = bit_of(axis, bit) == 0
        value = jnp.where(lower, jnp.concatenate([value, got], 0), jnp.concatenate([got, value], 0))
    return value


def routes():
    others, bit = [], 2
    while bit < lax.axis_size("dp"):
        others.append(("dp", bit))
        bit *= 2
    return [("dp", 1), ("seq", 2)] + others, [("seq", 2), ("dp", 1)] + others


def summed(keep, send):
    count = keep.shape[0]
    width = keep.shape[-1]
    local = (keep + swap(send, "seq", 1)).reshape(-1, width)
    half = local.shape[0] // 2
    pieces = [doubling(halving(local[i * half : (i + 1) * half], route), route) for i, route in enumerate(routes())]
    mine = jnp.concatenate(pieces, 0).reshape(count, -1, width)
    return mine, swap(mine, "seq", 1)


def butterfly(value):
    steps = [("seq", 1), ("seq", 2)]
    bit = 1
    while bit < lax.axis_size("dp"):
        steps.append(("dp", bit))
        bit *= 2
    for axis, bit in steps:
        value = value + swap(value, axis, bit)
    return value


def per_device(
    canvas,
    memory,
    canvas_len,
    memory_len,
    slot_cot,
    self_project,
    self_output,
    self_biases,
    cross_project,
    cross_output,
    cross_biases,
    norm_gains,
    norm_shifts,
    inner_weight,
    inner_bias,
    outer_weight,
    outer_bias,
    slot_weight,
    slot_bias,
):
    block, width = canvas.shape[2:]
    seat = lax.axis_index("seq")
    batch = seat // 2
    upper = batch == 1
    even = seat % 2 == 0

    def gather_rows(value):
        kept = jnp.where(upper, value[1, 0], value[0, 0])
        sent = jnp.where(upper, value[0, 0], value[1, 0])
        return jnp.concatenate([kept, swap(sent, "seq", 2)], 0)

    def whole_rows(rows):
        return jnp.concatenate([rows, swap(rows, "seq", 1)], 0)

    def give_back(kept, sent):
        got = swap(sent, "seq", 2).astype(kept.dtype)
        return jnp.where(upper, jnp.stack([got, kept]), jnp.stack([kept, got]))[:, None]

    scalars = jnp.stack(
        [
            seat.astype(jnp.int32),
            jnp.where(upper, canvas_len[1, 0], canvas_len[0, 0]),
            jnp.where(upper, memory_len[1, 0], memory_len[0, 0]),
        ]
    )
    rows = gather_rows(canvas)
    every = whole_rows(rows)
    source = gather_rows(memory)
    source_every = whole_rows(source)
    cotangent = gather_rows(slot_cot)
    cot_halo = swap(jnp.stack([cotangent[block - 1], cotangent[2 * block - 1]]), "seq", 1)

    q, k, v, p, o, inverse, normal_one, spread_one = attention_forward(
        False, scalars, rows, every, self_project, self_biases, self_output, norm_gains, norm_shifts
    )
    low_one, q2, k2, v2, p2, o2, inverse2, normal_two, spread_two = attention_forward(
        True, scalars, normal_one, source_every, cross_project, cross_biases, cross_output, norm_gains, norm_shifts
    )
    feed_keep, feed_send, state, grad_two, small_feed = feed_forward(
        scalars, normal_two, norm_gains, norm_shifts, cotangent, cot_halo, inner_weight, inner_bias,
        outer_weight, outer_bias, slot_weight,
    )
    cross_keep, cross_send, small_cross, grad_one, memory_own, memory_other = attention_backward(
        True, scalars, grad_two, normal_two, spread_two, norm_gains, o2, inverse2, q2, k2, v2, p2,
        low_one, source_every, cross_project, cross_output,
    )
    self_keep, self_send, small_self, canvas_own, _, canvas_other = attention_backward(
        False, scalars, grad_one, normal_one, spread_one, norm_gains, o, inverse, q, k, v, p,
        rows, every, self_project, self_output,
    )

    state_halo = swap(jnp.stack([state[0], state[block]]), "seq", 1)
    slots = slot_states(scalars, state, state_halo, slot_weight, slot_bias)
    slots_out = give_back(slots[:block], slots[block:])

    memory_total = memory_own.astype(F32) + swap(memory_other, "seq", 1).astype(F32)
    memory_out = give_back(memory_total[:block], memory_total[block:].astype(BF16))
    canvas_total = canvas_own + swap(canvas_other, "seq", 1).astype(F32)
    canvas_out = give_back(canvas_total[:block], canvas_total[block:].astype(BF16))

    def ordered(keep, send):
        mine, other = summed(keep, send)
        first = jnp.where(even, mine, other).astype(F32)
        second = jnp.where(even, other, mine).astype(F32)
        return first, second

    feed_first, feed_second = ordered(feed_keep, feed_send)
    cross_first, cross_second = ordered(cross_keep, cross_send)
    self_first, self_second = ordered(self_keep, self_send)
    small = butterfly(jnp.concatenate([small_feed, small_cross, small_self], 0))
    grad_slot = jnp.concatenate([feed_first[0], feed_second[0]], 0)
    grad_outer = feed_first[1:].reshape(outer_weight.shape)
    grad_inner = jnp.concatenate([feed_second[i] for i in range(1, feed_second.shape[0])], 1)
    hidden_parts = inner_bias.shape[0] // width
    return (
        slots_out,
        canvas_out,
        memory_out,
        jnp.stack([self_first[1], self_second[0], self_second[1]]),
        self_first[0],
        jnp.stack([small[19], small[20], small[18]]),
        jnp.stack([cross_first[1], cross_second[0], cross_second[1]]),
        cross_first[0],
        jnp.stack([small[11], small[12], small[10]]),
        jnp.stack([small[16], small[8], small[1]]),
        jnp.stack([small[17], small[9], small[2]]),
        grad_inner,
        small[4 : 4 + hidden_parts].reshape(-1),
        grad_outer,
        small[3],
        grad_slot,
        small[0],
    )


def solution(mesh):
    tokens = P(None, "dp", "seq", None)
    sizes = P(None, "dp")
    return jax.shard_map(
        per_device,
        mesh=mesh,
        in_specs=(tokens, tokens, sizes, sizes, tokens) + (P(),) * 14,
        out_specs=(tokens,) * 3 + (P(),) * 14,
        check_vma=False,
    )
```

```python
import functools

import jax
import jax.numpy as jnp
from jax import lax
from jax.experimental import pallas as pl
from jax.experimental.pallas import tpu as pltpu
from jax.sharding import PartitionSpec as P

LANES = 128
CHUNK = 256
EPSILON = 1e-05
MASKED = -1e30
VMEM_LIMIT = 60 << 20
F32 = jnp.float32
BF16 = jnp.bfloat16
BLOCKS = (0, 2, 1, 3)


def product(left, right):
    return jnp.dot(left, right, preferred_element_type=F32)


def left_product(left, right):
    return lax.dot_general(left, right, (((0,), (0,)), ((), ())), preferred_element_type=F32)


def right_product(left, right):
    return lax.dot_general(left, right, (((1,), (1,)), ((), ())), preferred_element_type=F32)


def column_sum(value):
    return jnp.sum(value, 0, keepdims=True)


def norm_forward(value):
    mean = jnp.mean(value, -1, keepdims=True)
    centered = value - mean
    spread = jnp.mean(centered * centered, -1, keepdims=True)
    inverse = lax.rsqrt(spread + EPSILON)
    return centered * inverse, inverse


def norm_backward(upstream, normal, inverse, gain):
    scaled = upstream * gain
    inner_mean = jnp.mean(scaled, -1, keepdims=True)
    cross_mean = jnp.mean(scaled * normal, -1, keepdims=True)
    return inverse * (scaled - inner_mean - normal * cross_mean)


def wide_row(ref, row):
    return ref[row : row + 1, :].astype(F32)


def head_only(value, which):
    lane = lax.broadcasted_iota(jnp.int32, (1, LANES), 1)
    mine = lane < LANES // 2 if which == 0 else lane >= LANES // 2
    return jnp.where(mine, value, jnp.zeros_like(value))


def head_pick(first, second):
    lane = lax.broadcasted_iota(jnp.int32, (1, LANES), 1)
    return jnp.where(lane < LANES // 2, first, second)


def pair_of(step):
    return pl.ds(pl.multiple_of(step * LANES, LANES), LANES)


def forward_body(cross, scalars, *refs):
    if cross:
        rows_in, *refs = refs
    all_in, refs = refs[: len(BLOCKS)], refs[len(BLOCKS) :]
    project, biases, wo, gains, shifts, *refs = refs
    if cross:
        out_low, *refs = refs
    out_q, out_k, out_v, out_p, out_o, out_inverse, out_normal, out_spread = refs[:8]
    every, queries, both_all = refs[8:]
    step = pl.program_id(0)
    block = all_in[0].shape[0]
    width = every.shape[1]
    rows, total = 2 * block, len(BLOCKS) * block
    seat, size = scalars[0], scalars[2 if cross else 1]

    @pl.when(step == 0)
    def _():
        for index, ref in enumerate(all_in):
            every[index * block : (index + 1) * block, :] = ref[...]
        if cross:
            value = rows_in[...] * wide_row(gains, 0) + wide_row(shifts, 0)
            out_low[...] = value.astype(BF16)
            source = out_low[...]
        else:
            source = every[:rows, :]
        query = product(source, project[0]) + wide_row(biases, 0)
        queries[...] = query.astype(BF16) * jnp.asarray(0.125, BF16)
        both_all[0] = product(every[...], project[1]).astype(BF16)
        both_all[1] = (product(every[...], project[2]) + wide_row(biases, 1)).astype(BF16)

    query = queries[:, pair_of(step)]
    keys = both_all[0, :, pair_of(step)]
    values = both_all[1, :, pair_of(step)]
    out_q[...] = query
    out_k[...] = keys
    out_v[...] = values
    wide = jnp.concatenate([values, jnp.ones((total, LANES), BF16)], 1)
    place = lax.broadcasted_iota(jnp.int32, (1, block), 1)
    bias = jnp.concatenate(
        [jnp.where((seat ^ item) * block + place < size, 0.0, MASKED) for item in BLOCKS], 1
    )
    for start in range(0, rows, CHUNK):
        piece = query[start : start + CHUNK]
        parts = []
        for head in range(2):
            scores = right_product(head_only(piece, head), keys) + bias
            weights = jnp.exp(scores - jnp.max(scores, 1, keepdims=True)).astype(BF16)
            out_p[head, start : start + CHUNK, :] = weights
            result = product(weights, wide)
            inverse = 1.0 / result[:, LANES:]
            parts.append((result[:, :LANES] * inverse, inverse))
        out_o[start : start + CHUNK, pair_of(step)] = head_pick(parts[0][0], parts[1][0]).astype(BF16)
        out_inverse[start : start + CHUNK, pair_of(step)] = head_pick(parts[0][1], parts[1][1]).astype(BF16)

    @pl.when(step == pl.num_programs(0) - 1)
    def _():
        if cross:
            base = rows_in[...] * wide_row(gains, 0) + wide_row(shifts, 0)
        else:
            base = every[:rows, :].astype(F32)
        value = base + product(out_o[...], wo[...]) + wide_row(biases, 2)
        normal, inverse = norm_forward(value)
        out_normal[...] = normal
        out_spread[...] = jnp.broadcast_to(inverse, out_spread.shape)


def whole(*shape):
    return pl.BlockSpec(shape, lambda i: (0,) * len(shape))


SMEM = pl.BlockSpec(memory_space=pltpu.SMEM)
LATER = pl.BlockSpec(memory_space=pl.ANY)


def attention_forward(cross, scalars, rows_in, all_in, project, biases, wo, gains, shifts):
    block, width = all_in[0].shape
    rows, total = 2 * block, len(BLOCKS) * block
    pairs = width // LANES
    part = lambda count: pl.BlockSpec((count, LANES), lambda i: (0, i))
    out_shape = [
        jax.ShapeDtypeStruct((rows, width), BF16),
        jax.ShapeDtypeStruct((total, width), BF16),
        jax.ShapeDtypeStruct((total, width), BF16),
        jax.ShapeDtypeStruct((2 * pairs, rows, total), BF16),
        jax.ShapeDtypeStruct((rows, width), BF16),
        jax.ShapeDtypeStruct((rows, width), BF16),
        jax.ShapeDtypeStruct((rows, width), F32),
        jax.ShapeDtypeStruct((rows, LANES), F32),
    ]
    out_specs = [
        part(rows),
        part(total),
        part(total),
        pl.BlockSpec((2, rows, total), lambda i: (i, 0, 0)),
        whole(rows, width),
        whole(rows, width),
        whole(rows, width),
        whole(rows, LANES),
    ]
    if cross:
        out_shape = [jax.ShapeDtypeStruct((rows, width), BF16)] + out_shape
        out_specs = [whole(rows, width)] + out_specs
    return pl.pallas_call(
        functools.partial(forward_body, cross),
        grid=(pairs,),
        in_specs=[SMEM]
        + ([whole(rows, width)] if cross else [])
        + [whole(block, width)] * len(BLOCKS)
        + [whole(3, width, width), whole(3, width), whole(width, width), whole(3, width), whole(3, width)],
        out_specs=out_specs,
        out_shape=out_shape,
        scratch_shapes=[
            pltpu.VMEM((total, width), BF16),
            pltpu.VMEM((rows, width), BF16),
            pltpu.VMEM((2, total, width), BF16),
        ],
        compiler_params=pltpu.CompilerParams(vmem_limit_bytes=VMEM_LIMIT),
        cost_estimate=pl.CostEstimate(
            flops=2 * rows * total * width * 8, bytes_accessed=20 << 20, transcendentals=rows * total * 8
        ),
        name="cross_forward" if cross else "self_forward",
    )(scalars, *([rows_in] if cross else []), *all_in, project, biases, wo, gains, shifts)


def backward_body(cross, *refs):
    if cross:
        upstream_in, *refs = refs
    else:
        base_in, query_two, wq, *refs = refs
    normal, spread, gains, inverse, wo, mixed, query, keys, values, weights = refs[:10]
    out_query, out_key, out_value, out_small, out_rows, mixed_grad = refs[-6:]
    step = pl.program_id(0)
    rows, width = mixed.shape
    total = keys.shape[0]
    pair = pair_of(step)

    @pl.when(step == 0)
    def _():
        out_small[...] = jnp.zeros(out_small.shape, F32)
        if cross:
            upstream = upstream_in[...]
        else:
            upstream = base_in[...] + right_product(query_two[...], wq[0])
        normal_now = normal[...]
        grad = norm_backward(upstream, normal_now, spread[:, 0:1], wide_row(gains, 1 if cross else 0))
        out_small[0:1, :] = column_sum(upstream * normal_now)
        out_small[1:2, :] = column_sum(upstream)
        out_small[2:3, :] = column_sum(grad)
        out_rows[...] = grad
        mixed_grad[...] = (right_product(grad.astype(BF16), wo[...]) * inverse[...].astype(F32)).astype(BF16)

    keys_now, values_now = keys[...], values[...]
    key_grad = jnp.zeros((LANES, total), F32)
    value_grad = jnp.zeros((LANES, total), F32)
    query_grads = []
    for start in range(0, rows, CHUNK):
        span = slice(start, start + CHUNK)
        piece = query[span, :]
        grad = mixed_grad[span, pair]
        center = grad.astype(F32) * mixed[span, pair].astype(F32)
        found = []
        for head in range(2):
            grad_now = head_only(grad, head)
            center_now = jnp.sum(head_only(center, head), 1, keepdims=True)
            weight = weights[head, span, :]
            slope = right_product(grad_now, values_now)
            score_grad = (weight.astype(F32) * (slope - center_now)).astype(BF16)
            found.append(product(score_grad, keys_now))
            value_grad = value_grad + left_product(grad_now, weight)
            key_grad = key_grad + left_product(head_only(piece, head), score_grad)
        query_grads.append(head_pick(found[0], found[1]) * 0.125)
    query_grad = jnp.concatenate(query_grads, 0)
    value_grad = value_grad.T
    out_small[3:4, pair] = column_sum(query_grad)
    out_small[4:5, pair] = column_sum(value_grad)
    out_query[...] = query_grad.astype(BF16)
    out_key[...] = key_grad.T.astype(BF16)
    out_value[...] = value_grad.astype(BF16)


def attention_backward(cross, first_inputs, mixed, query, keys, values, weights, later=()):
    rows, width = mixed.shape
    total = keys.shape[0]
    pairs = width // LANES
    part = lambda count: pl.BlockSpec((count, LANES), lambda i: (0, i))
    front = [whole(1, *value.shape[1:]) if value.ndim == 3 else whole(*value.shape) for value in first_inputs]
    return pl.pallas_call(
        functools.partial(backward_body, cross),
        grid=(pairs,),
        in_specs=front
        + [whole(rows, width), part(rows), part(total), part(total)]
        + [pl.BlockSpec((2, rows, total), lambda i: (i, 0, 0))]
        + [LATER] * len(later),
        out_specs=[part(rows), part(total), part(total), whole(8, width), whole(rows, width)],
        out_shape=[
            jax.ShapeDtypeStruct((rows, width), BF16),
            jax.ShapeDtypeStruct((total, width), BF16),
            jax.ShapeDtypeStruct((total, width), BF16),
            jax.ShapeDtypeStruct((8, width), F32),
            jax.ShapeDtypeStruct((rows, width), F32),
        ],
        scratch_shapes=[pltpu.VMEM((rows, width), BF16)],
        compiler_params=pltpu.CompilerParams(vmem_limit_bytes=VMEM_LIMIT),
        cost_estimate=pl.CostEstimate(
            flops=2 * rows * total * width * 16, bytes_accessed=20 << 20, transcendentals=0
        ),
        name="cross_backward" if cross else "self_backward",
    )(*first_inputs, mixed, query, keys, values, weights, *later)


def weights_body(cross, scalars, *refs):
    mixed, grad_in, rows_in, *refs = refs
    all_in, refs = refs[: len(BLOCKS)], refs[len(BLOCKS) :]
    query_in, key_in, value_in, project = refs[:4]
    if cross:
        slot_keep, slot_send = refs[4:6]
    out_keep, out_send, out_own, out_other = refs[-4:]
    rows = mixed.shape[0]
    even = lax.rem(scalars[0], 2) == 0
    query_grad, key_grad, value_grad = query_in[...], key_in[...], value_in[...]

    def store(kept_by_even, index, value):
        value = value.astype(BF16)

        @pl.when(even if kept_by_even else jnp.logical_not(even))
        def _():
            out_keep[index] = value

        @pl.when(jnp.logical_not(even) if kept_by_even else even)
        def _():
            out_send[index] = value

    if cross:
        out_keep[2] = slot_keep[...]
        out_send[2] = slot_send[...]
    every = jnp.concatenate([ref[...] for ref in all_in], 0)
    grad = grad_in[...]
    store(True, 0, left_product(mixed[...], grad.astype(BF16)))
    store(True, 1, left_product(rows_in[...] if cross else every[:rows, :], query_grad))
    store(False, 0, left_product(every, key_grad))
    store(False, 1, left_product(every, value_grad))
    spread_out = right_product(key_grad, project[1]) + right_product(value_grad, project[2])
    own = spread_out[:rows, :]
    if not cross:
        own = own + grad + right_product(query_grad, project[0])
    out_own[...] = own
    out_other[...] = spread_out[rows:, :].astype(BF16)


VMEM = pl.BlockSpec(memory_space=pltpu.VMEM)


def weight_gradients(cross, scalars, mixed, grad, rows_in, all_in, grads, project, slots=(), later=()):
    block, width = all_in[0].shape
    rows, total = 2 * block, len(BLOCKS) * block
    count = 3 if cross else 2
    return pl.pallas_call(
        functools.partial(weights_body, cross),
        in_specs=[SMEM] + [VMEM] * (3 + len(BLOCKS) + 3 + 1 + len(slots)) + [LATER] * len(later),
        out_specs=[VMEM] * 4,
        out_shape=[
            jax.ShapeDtypeStruct((count, width, width), BF16),
            jax.ShapeDtypeStruct((count, width, width), BF16),
            jax.ShapeDtypeStruct((rows, width), F32),
            jax.ShapeDtypeStruct((total - rows, width), BF16),
        ],
        compiler_params=pltpu.CompilerParams(vmem_limit_bytes=VMEM_LIMIT),
        cost_estimate=pl.CostEstimate(flops=24 * rows * width * width, bytes_accessed=12 << 20, transcendentals=0),
        name="cross_weights" if cross else "self_weights",
    )(scalars, mixed, grad, rows_in, *all_in, *grads, project, *slots, *later)


SPLIT = 2


def gelu(value):
    square = value * value
    bent = jnp.tanh(0.7978845608028654 * value * (1.0 + 0.044715 * square))
    half = 0.5 * (1.0 + bent)
    slope = half + 0.5 * value * (1.0 - bent * bent) * (0.7978845608028654 + 3 * 0.044715 * 0.7978845608028654 * square)
    return value * half, slope


def feed_body(scalars, normal_two, gains, shifts, cot_one, cot_two, halo, wi, bi, wo, bo, slot_weight,
              out_keep, out_send, out_slot_keep, out_slot_send, out_state, out_grad, out_small,
              low, slopes, active, acc, low_grad):
    step = pl.program_id(0)
    rows, width = normal_two.shape
    block = rows // 2
    span = wi.shape[1]
    seat, size = scalars[0], scalars[1]
    even = lax.rem(seat, 2) == 0

    def store(kept_by_even, keep, send, index, value):
        value = value.astype(BF16)

        @pl.when(even if kept_by_even else jnp.logical_not(even))
        def _():
            keep[index] = value

        @pl.when(jnp.logical_not(even) if kept_by_even else even)
        def _():
            send[index] = value

    @pl.when(step == 0)
    def _():
        value = normal_two[...] * wide_row(gains, 1) + wide_row(shifts, 1)
        low[...] = value.astype(BF16)
        acc[...] = value + bo[...].astype(F32)

    @pl.when(step < SPLIT)
    def _():
        start = step * span
        for part in range(0, span, width):
            value = product(low[...], wi[:, part : part + width]) + bi[:, part : part + width].astype(F32)
            found, slope = gelu(value)
            place = pl.ds(pl.multiple_of(start + part, width), width)
            slopes[:, place] = slope
            active[:, place] = found.astype(BF16)
        acc[...] += product(active[:, pl.ds(pl.multiple_of(start, span), span)], wo[...])

    @pl.when(step == SPLIT)
    def _():
        normal, inverse = norm_forward(acc[...])
        state = (normal * wide_row(gains, 2) + wide_row(shifts, 2)).astype(BF16)
        out_state[...] = state
        out_small[...] = jnp.zeros(out_small.shape, F32)
        place = lax.broadcasted_iota(jnp.int32, (block, 1), 0)
        sides = []
        for index, (item, cot) in enumerate(zip(BLOCKS[:2], (cot_one, cot_two))):
            first = (seat ^ item) * block
            value = cot[...].astype(F32)
            straight = jnp.where(first + place + 1 < size, value, 0.0)
            before = jnp.where(even, wide_row(halo, 1 - index), wide_row(halo, index))
            moved = jnp.where(place == 0, before, pltpu.roll(value, 1, 0))
            moved = jnp.where((first + place < size) & (first + place > 0), moved, 0.0)
            sides.append(jnp.concatenate([straight, moved], 1))
        sides = jnp.concatenate(sides, 0)
        out_small[0:1, :] = column_sum(sides[:, :width])
        sides = sides.astype(BF16)
        slot_grad = left_product(state, sides)
        store(True, out_slot_keep, out_slot_send, slice(None), slot_grad[:, :width])
        store(False, out_slot_keep, out_slot_send, slice(None), slot_grad[:, width:])
        state_grad = right_product(
            sides, jnp.concatenate([slot_weight[:width, :], slot_weight[width:, :]], 1)
        )
        out_small[1:2, :] = column_sum(state_grad * normal)
        out_small[2:3, :] = column_sum(state_grad)
        grad = norm_backward(state_grad, normal, inverse, wide_row(gains, 2))
        out_small[3:4, :] = column_sum(grad)
        acc[...] = grad
        low_grad[...] = grad.astype(BF16)

    @pl.when(step > SPLIT)
    def _():
        start = (step - SPLIT - 1) * span
        found = []
        for part in range(0, span, width):
            place = pl.ds(pl.multiple_of(start + part, width), width)
            grad = right_product(low_grad[...], wo[part : part + width, :]) * slopes[:, place]
            out_small[pl.ds(4 + (step - SPLIT - 1) * (span // width) + part // width, 1), :] = column_sum(grad)
            grad_low = grad.astype(BF16)
            found.append(grad_low)
            store(True, out_keep, out_send, part // width, left_product(active[:, place], low_grad[...]))
            store(False, out_keep, out_send, part // width, left_product(low[...], grad_low))
        acc[...] += right_product(jnp.concatenate(found, 1), wi[...])

    @pl.when(step == pl.num_programs(0) - 1)
    def _():
        out_grad[...] = acc[...]


def feed_forward(scalars, normal_two, gains, shifts, cots, halo, wi, bi, wo, bo, slot_weight):
    rows, width = normal_two.shape
    hidden = wi.shape[1]
    span = hidden // SPLIT
    part = lambda i: jnp.where(i < SPLIT, i, jnp.maximum(i - SPLIT - 1, 0))
    group = pl.BlockSpec((span // width, width, width), lambda i: (jnp.maximum(i - SPLIT - 1, 0), 0, 0))
    grads = jax.ShapeDtypeStruct((hidden // width, width, width), BF16)
    slot = jax.ShapeDtypeStruct((width, width), BF16)
    return pl.pallas_call(
        feed_body,
        grid=(2 * SPLIT + 1,),
        in_specs=[
            SMEM,
            whole(rows, width),
            whole(3, width),
            whole(3, width),
            whole(rows // 2, width),
            whole(rows // 2, width),
            whole(2, width),
            pl.BlockSpec((width, span), lambda i: (0, part(i))),
            pl.BlockSpec((1, span), lambda i: (0, part(i))),
            pl.BlockSpec((span, width), lambda i: (part(i), 0)),
            whole(1, width),
            whole(2 * width, width),
        ],
        out_specs=[group, group, whole(width, width), whole(width, width), whole(rows, width), whole(rows, width),
                   whole(8, width)],
        out_shape=[
            grads,
            grads,
            slot,
            slot,
            jax.ShapeDtypeStruct((rows, width), BF16),
            jax.ShapeDtypeStruct((rows, width), F32),
            jax.ShapeDtypeStruct((8, width), F32),
        ],
        scratch_shapes=[
            pltpu.VMEM((rows, width), BF16),
            pltpu.VMEM((rows, hidden), F32),
            pltpu.VMEM((rows, hidden), BF16),
            pltpu.VMEM((rows, width), F32),
            pltpu.VMEM((rows, width), BF16),
        ],
        compiler_params=pltpu.CompilerParams(vmem_limit_bytes=VMEM_LIMIT),
        cost_estimate=pl.CostEstimate(
            flops=2 * rows * width * width * 32, bytes_accessed=20 << 20, transcendentals=rows * width * 8
        ),
        name="feed_forward",
    )(scalars, normal_two, gains, shifts, *cots, halo, wi, bi.reshape(1, -1), wo, bo.reshape(1, -1), slot_weight)


def slot_body(scalars, state, halo, slot_weight, slot_bias, out):
    rows, width = state.shape
    block = rows // 2
    seat, size = scalars[0], scalars[1]
    even = lax.rem(seat, 2) == 0
    place = lax.broadcasted_iota(jnp.int32, (block, 1), 0)
    for index, item in enumerate(BLOCKS[:2]):
        span = slice(index * block, (index + 1) * block)
        value = state[span, :]
        after = jnp.where(even, wide_row(halo, index), wide_row(halo, 1 - index))
        moved = jnp.where(place == block - 1, after, pltpu.roll(value.astype(F32), block - 1, 0)).astype(BF16)
        result = product(value, slot_weight[:width, :]) + product(moved, slot_weight[width:, :])
        result = result + slot_bias[...].astype(F32)
        out[span, :] = jnp.where((seat ^ item) * block + place + 1 < size, result, 0.0).astype(BF16)


def slot_states(scalars, state, halo, slot_weight, slot_bias):
    rows, width = state.shape
    vmem = pl.BlockSpec(memory_space=pltpu.VMEM)
    return pl.pallas_call(
        slot_body,
        in_specs=[SMEM] + [vmem] * 4,
        out_specs=vmem,
        out_shape=jax.ShapeDtypeStruct((rows, width), BF16),
        compiler_params=pltpu.CompilerParams(vmem_limit_bytes=16 << 20),
        cost_estimate=pl.CostEstimate(flops=4 * rows * width * width, bytes_accessed=4 << 20, transcendentals=0),
        name="slot_states",
    )(scalars, state, halo, slot_weight, slot_bias.reshape(1, -1))


def feed_finish_body(scalars, mine, other, out_outer, out_inner):
    even = lax.rem(scalars[0], 2) == 0
    out_outer[...] = jnp.where(even, mine[0], other[0]).astype(F32)
    out_inner[...] = jnp.where(even, other[0], mine[0]).astype(F32)


def feed_finish(scalars, mine, other):
    count, width, _ = mine.shape
    part = pl.BlockSpec((1, width, width), lambda i: (i, 0, 0))
    return pl.pallas_call(
        feed_finish_body,
        grid=(count,),
        in_specs=[SMEM, part, part],
        out_specs=[
            pl.BlockSpec((width, width), lambda i: (i, 0)),
            pl.BlockSpec((width, width), lambda i: (0, i)),
        ],
        out_shape=[
            jax.ShapeDtypeStruct((count * width, width), F32),
            jax.ShapeDtypeStruct((width, count * width), F32),
        ],
        compiler_params=pltpu.CompilerParams(vmem_limit_bytes=VMEM_LIMIT),
        cost_estimate=pl.CostEstimate(flops=0, bytes_accessed=12 * count * width * width, transcendentals=0),
        name="feed_finish",
    )(scalars, mine, other)


def attention_finish_body(scalars, mine, other, out_output, out_project, *out_slot):
    even = lax.rem(scalars[0], 2) == 0
    first = jnp.where(even, mine[...], other[...]).astype(F32)
    second = jnp.where(even, other[...], mine[...]).astype(F32)
    out_output[...] = first[0]
    out_project[0] = first[1]
    out_project[1] = second[0]
    out_project[2] = second[1]
    if out_slot:
        out_slot[0][0] = first[2]
        out_slot[0][1] = second[2]


def attention_finish(scalars, mine, other):
    count, width, _ = mine.shape
    span = width // 2
    part = lambda count: pl.BlockSpec((count, span, width), lambda i: (0, i, 0))
    out_specs = [pl.BlockSpec((span, width), lambda i: (i, 0)), part(3)]
    out_shape = [jax.ShapeDtypeStruct((width, width), F32), jax.ShapeDtypeStruct((3, width, width), F32)]
    if count == 3:
        out_specs.append(part(2))
        out_shape.append(jax.ShapeDtypeStruct((2, width, width), F32))
    return pl.pallas_call(
        attention_finish_body,
        grid=(width // span,),
        in_specs=[SMEM, part(count), part(count)],
        out_specs=out_specs,
        out_shape=out_shape,
        compiler_params=pltpu.CompilerParams(vmem_limit_bytes=VMEM_LIMIT),
        cost_estimate=pl.CostEstimate(flops=0, bytes_accessed=12 * count * width * width, transcendentals=0),
        name="attention_finish",
    )(scalars, mine, other)


def gate(values, after):
    count = len(values)
    return pl.pallas_call(
        lambda *refs: None,
        in_specs=[LATER] * (count + len(after)),
        out_specs=[LATER] * count,
        out_shape=[jax.ShapeDtypeStruct(value.shape, value.dtype) for value in values],
        input_output_aliases={index: index for index in range(count)},
        name="gate",
    )(*values, *after)


def swap(value, axis, bit):
    count = lax.axis_size(axis)
    return lax.ppermute(value, axis, [(place, place ^ bit) for place in range(count)])


def bit_of(axis, bit):
    return (lax.axis_index(axis) // bit) % 2


def routes():
    rest, bit = [], 2
    while bit < lax.axis_size("dp"):
        rest.append(("dp", bit))
        bit *= 2
    across, along = ("dp", 1), ("seq", 2)
    return list(zip([across, along] + rest, [along, across] + rest))


def mixed_swap(value, step):
    if step[0] == step[1]:
        return swap(value, *step[0])
    groups, seats = lax.axis_size("dp"), lax.axis_size("seq")
    pairs = []
    for group in range(groups):
        for seat in range(seats):
            axis, bit = step[seat % 2]
            target = (group ^ bit, seat) if axis == "dp" else (group, seat ^ bit)
            pairs.append((group * seats + seat, target[0] * seats + target[1]))
    return lax.ppermute(value, ("dp", "seq"), pairs)


def mixed_bit(step):
    if step[0] == step[1]:
        return bit_of(*step[0])
    return jnp.where(lax.axis_index("seq") % 2 == 0, bit_of(*step[0]), bit_of(*step[1]))


class Sum:
    def __init__(self, keep, got):
        self.shape = keep.shape
        self.terms = [keep.reshape(-1, keep.shape[-1]), got.reshape(-1, keep.shape[-1])]
        self.steps = routes()

    def halve(self, index, after=()):
        step = self.steps[index]
        half = self.terms[0].shape[0] // 2
        mine = mixed_bit(step) * half
        cut = lambda start: sum(lax.dynamic_slice_in_dim(term, start, half, 0) for term in self.terms)
        sent = cut(half - mine)
        if after:
            (sent,) = gate([sent], after)
        self.terms = [cut(mine), mixed_swap(sent, step)]
        return sent

    def double(self, index):
        step = self.steps[index]
        value = sum(self.terms)
        got = mixed_swap(value, step)
        lower = mixed_bit(step) == 0
        self.terms = [jnp.where(lower, jnp.concatenate([value, got], 0), jnp.concatenate([got, value], 0))]

    def finish(self):
        mine = self.terms[0].reshape(self.shape)
        return mine, swap(mine, "seq", 1)

    def rest(self, done=0):
        for index in range(done, len(self.steps)):
            self.halve(index)
        for index in reversed(range(len(self.steps))):
            self.double(index)
        return self.finish()


def butterfly(value):
    steps = [("seq", 1), ("seq", 2)]
    bit = 1
    while bit < lax.axis_size("dp"):
        steps.append(("dp", bit))
        bit *= 2
    for axis, bit in steps:
        value = value + swap(value, axis, bit)
    return value


def per_device(
    canvas,
    memory,
    canvas_len,
    memory_len,
    slot_cot,
    self_project,
    self_output,
    self_biases,
    cross_project,
    cross_output,
    cross_biases,
    norm_gains,
    norm_shifts,
    inner_weight,
    inner_bias,
    outer_weight,
    outer_bias,
    slot_weight,
    slot_bias,
):
    block, width = canvas.shape[2:]
    seat = lax.axis_index("seq")
    batch = seat // 2
    upper = batch == 1

    def own_of(value, index):
        return lax.dynamic_index_in_dim(value, index, 0, keepdims=False)

    def placed(kept, got):
        got = got.astype(kept.dtype)
        return jnp.where(upper, jnp.stack([got, kept]), jnp.stack([kept, got]))[:, None]

    kept, away = own_of(canvas, batch)[0], own_of(canvas, 1 - batch)[0]
    got = swap(away, "seq", 2)
    every = [kept, got, swap(kept, "seq", 1), swap(got, "seq", 1)]
    kept, away = own_of(memory, batch)[0], own_of(memory, 1 - batch)[0]
    source_every = [kept, swap(away, "seq", 2), swap(kept, "seq", 1), swap(away, "seq", 3)]
    cots = [own_of(slot_cot, batch)[0], swap(own_of(slot_cot, 1 - batch)[0], "seq", 2)]
    scalars = jnp.stack(
        [seat.astype(jnp.int32), own_of(canvas_len, batch)[0], own_of(memory_len, batch)[0]]
    )

    q, k, v, p, o, inverse, normal_one, spread_one = attention_forward(
        False, scalars, None, every, self_project, self_biases, self_output, norm_gains, norm_shifts
    )
    low_one, q2, k2, v2, p2, o2, inverse2, normal_two, spread_two = attention_forward(
        True, scalars, normal_one, source_every, cross_project, cross_biases, cross_output, norm_gains, norm_shifts
    )
    cot_halo = swap(jnp.stack([cot[block - 1] for cot in cots]), "seq", 1)
    feed_keep, feed_send, slot_keep, slot_send, state, grad_two, small_feed = feed_forward(
        scalars, normal_two, norm_gains, norm_shifts, cots, cot_halo, inner_weight, inner_bias,
        outer_weight, outer_bias, slot_weight,
    )

    feed = Sum(feed_keep, swap(feed_send, "seq", 1))
    state_halo = swap(jnp.stack([state[0], state[block]]), "seq", 1)
    dq2, dk2, dv2, small_cross, grad_mid = attention_backward(
        True, [grad_two, normal_two, spread_two, norm_gains, inverse2, cross_output], o2, q2, k2, v2, p2
    )
    sent = feed.halve(0, [dq2])
    cross_keep, cross_send, memory_own, memory_other = weight_gradients(
        True, scalars, o2, grad_mid, low_one, source_every, [dq2, dk2, dv2], cross_project,
        slots=[slot_keep, slot_send], later=[sent]
    )
    cross = Sum(cross_keep, swap(cross_send, "seq", 1))
    dq, dk, dv, small_self, grad_first = attention_backward(
        False, [grad_mid, dq2, cross_project, normal_one, spread_one, norm_gains, inverse, self_output],
        o, q, k, v, p, later=[cross_send],
    )
    sent = feed.halve(1)
    self_keep, self_send, canvas_own, canvas_other = weight_gradients(
        False, scalars, o, grad_first, every[0], every, [dq, dk, dv], self_project, later=[sent]
    )
    own = Sum(self_keep, swap(self_send, "seq", 1))

    slots = slot_states(scalars, state, state_halo, slot_weight, slot_bias)
    memory_total = memory_own + swap(memory_other, "seq", 1).astype(F32)
    canvas_total = canvas_own + swap(canvas_other, "seq", 1).astype(F32)
    (small,) = gate([jnp.concatenate([small_feed, small_cross, small_self], 0)], [self_keep])
    small = butterfly(small)

    grad_outer, grad_inner = feed_finish(scalars, *feed.rest(2))
    grad_cross_output, grad_cross_project, grad_slot = attention_finish(scalars, *cross.rest())
    grad_self_output, grad_self_project = attention_finish(scalars, *own.rest())

    hidden_parts = inner_bias.shape[0] // width
    return (
        placed(slots[:block], swap(slots[block:], "seq", 2)),
        placed(canvas_total[:block], swap(canvas_total[block:].astype(BF16), "seq", 2)),
        placed(memory_total[:block], swap(memory_total[block:].astype(BF16), "seq", 2)),
        grad_self_project,
        grad_self_output,
        jnp.stack([small[19], small[20], small[18]]),
        grad_cross_project,
        grad_cross_output,
        jnp.stack([small[11], small[12], small[10]]),
        jnp.stack([small[16], small[8], small[1]]),
        jnp.stack([small[17], small[9], small[2]]),
        grad_inner,
        small[4 : 4 + hidden_parts].reshape(-1),
        grad_outer,
        small[3],
        grad_slot.reshape(slot_weight.shape),
        small[0],
    )


def solution(mesh):
    tokens = P(None, "dp", "seq", None)
    sizes = P(None, "dp")
    return jax.shard_map(
        per_device,
        mesh=mesh,
        in_specs=(tokens, tokens, sizes, sizes, tokens) + (P(),) * 14,
        out_specs=(tokens,) * 3 + (P(),) * 14,
        check_vma=False,
    )
```

```python
import functools

import jax
import jax.numpy as jnp
from jax import lax
from jax.experimental import pallas as pl
from jax.experimental.pallas import tpu as pltpu
from jax.sharding import PartitionSpec as P

LANES = 128
CHUNK = 256
SMALL = 128
EPSILON = 1e-05
MASKED = -1e30
VMEM_LIMIT = 60 << 20
F32 = jnp.float32
BF16 = jnp.bfloat16
BLOCKS = (0, 2, 1, 3)


def product(left, right):
    return jnp.dot(left, right, preferred_element_type=F32)


def left_product(left, right):
    return lax.dot_general(left, right, (((0,), (0,)), ((), ())), preferred_element_type=F32)


def right_product(left, right):
    return lax.dot_general(left, right, (((1,), (1,)), ((), ())), preferred_element_type=F32)


def column_sum(value):
    return jnp.sum(value, 0, keepdims=True)


def norm_forward(value):
    mean = jnp.mean(value, -1, keepdims=True)
    centered = value - mean
    spread = jnp.mean(centered * centered, -1, keepdims=True)
    inverse = lax.rsqrt(spread + EPSILON)
    return centered * inverse, inverse


def norm_backward(upstream, normal, inverse, gain):
    scaled = upstream * gain
    inner_mean = jnp.mean(scaled, -1, keepdims=True)
    cross_mean = jnp.mean(scaled * normal, -1, keepdims=True)
    return inverse * (scaled - inner_mean - normal * cross_mean)


def wide_row(ref, row):
    return ref[row : row + 1, :].astype(F32)


def head_only(value, which):
    lane = lax.broadcasted_iota(jnp.int32, (1, LANES), 1)
    mine = lane < LANES // 2 if which == 0 else lane >= LANES // 2
    return jnp.where(mine, value, jnp.zeros_like(value))


def head_pick(first, second):
    lane = lax.broadcasted_iota(jnp.int32, (1, LANES), 1)
    return jnp.where(lane < LANES // 2, first, second)


def pair_of(step):
    return pl.ds(pl.multiple_of(step * LANES, LANES), LANES)


def forward_body(cross, scalars, *refs):
    if cross:
        rows_in, *refs = refs
    all_in, refs = refs[: len(BLOCKS)], refs[len(BLOCKS) :]
    project, biases, wo, gains, shifts, *refs = refs
    if cross:
        out_low, *refs = refs
    out_q, out_k, out_v, out_p, out_o, out_inverse, out_normal, out_spread = refs[:8]
    every, queries, both_all = refs[8:]
    step = pl.program_id(0)
    block = all_in[0].shape[0]
    width = every.shape[1]
    rows, total = 2 * block, len(BLOCKS) * block
    seat, size = scalars[0], scalars[2 if cross else 1]

    @pl.when(step == 0)
    def _():
        for index, ref in enumerate(all_in):
            every[index * block : (index + 1) * block, :] = ref[...]
        if cross:
            value = rows_in[...] * wide_row(gains, 0) + wide_row(shifts, 0)
            out_low[...] = value.astype(BF16)
            source = out_low[...]
        else:
            source = every[:rows, :]
        query = product(source, project[0]) + wide_row(biases, 0)
        queries[...] = query.astype(BF16) * jnp.asarray(0.125, BF16)
        both_all[0] = product(every[...], project[1]).astype(BF16)
        both_all[1] = (product(every[...], project[2]) + wide_row(biases, 1)).astype(BF16)

    query = queries[:, pair_of(step)]
    keys = both_all[0, :, pair_of(step)]
    values = both_all[1, :, pair_of(step)]
    out_q[...] = query
    out_k[...] = keys
    out_v[...] = values
    wide = jnp.concatenate([values, jnp.ones((total, LANES), BF16)], 1)
    place = lax.broadcasted_iota(jnp.int32, (1, block), 1)
    bias = jnp.concatenate(
        [jnp.where((seat ^ item) * block + place < size, 0.0, MASKED) for item in BLOCKS], 1
    )
    for start in range(0, rows, CHUNK):
        piece = query[start : start + CHUNK]
        parts = []
        for head in range(2):
            scores = right_product(head_only(piece, head), keys) + bias
            weights = jnp.exp(scores - jnp.max(scores, 1, keepdims=True)).astype(BF16)
            out_p[head, start : start + CHUNK, :] = weights
            result = product(weights, wide)
            inverse = 1.0 / result[:, LANES:]
            parts.append((result[:, :LANES] * inverse, inverse))
        out_o[start : start + CHUNK, pair_of(step)] = head_pick(parts[0][0], parts[1][0]).astype(BF16)
        out_inverse[start : start + CHUNK, pair_of(step)] = head_pick(parts[0][1], parts[1][1]).astype(BF16)

    @pl.when(step == pl.num_programs(0) - 1)
    def _():
        if cross:
            base = rows_in[...] * wide_row(gains, 0) + wide_row(shifts, 0)
        else:
            base = every[:rows, :].astype(F32)
        value = base + product(out_o[...], wo[...]) + wide_row(biases, 2)
        normal, inverse = norm_forward(value)
        out_normal[...] = normal
        out_spread[...] = jnp.broadcast_to(inverse, out_spread.shape)


def whole(*shape):
    return pl.BlockSpec(shape, lambda i: (0,) * len(shape))


SMEM = pl.BlockSpec(memory_space=pltpu.SMEM)
LATER = pl.BlockSpec(memory_space=pl.ANY)


def attention_forward(cross, scalars, rows_in, all_in, project, biases, wo, gains, shifts):
    block, width = all_in[0].shape
    rows, total = 2 * block, len(BLOCKS) * block
    pairs = width // LANES
    part = lambda count: pl.BlockSpec((count, LANES), lambda i: (0, i))
    out_shape = [
        jax.ShapeDtypeStruct((rows, width), BF16),
        jax.ShapeDtypeStruct((total, width), BF16),
        jax.ShapeDtypeStruct((total, width), BF16),
        jax.ShapeDtypeStruct((2 * pairs, rows, total), BF16),
        jax.ShapeDtypeStruct((rows, width), BF16),
        jax.ShapeDtypeStruct((rows, width), BF16),
        jax.ShapeDtypeStruct((rows, width), F32),
        jax.ShapeDtypeStruct((rows, LANES), F32),
    ]
    out_specs = [
        part(rows),
        part(total),
        part(total),
        pl.BlockSpec((2, rows, total), lambda i: (i, 0, 0)),
        whole(rows, width),
        whole(rows, width),
        whole(rows, width),
        whole(rows, LANES),
    ]
    if cross:
        out_shape = [jax.ShapeDtypeStruct((rows, width), BF16)] + out_shape
        out_specs = [whole(rows, width)] + out_specs
    return pl.pallas_call(
        functools.partial(forward_body, cross),
        grid=(pairs,),
        in_specs=[SMEM]
        + ([whole(rows, width)] if cross else [])
        + [whole(block, width)] * len(BLOCKS)
        + [whole(3, width, width), whole(3, width), whole(width, width), whole(3, width), whole(3, width)],
        out_specs=out_specs,
        out_shape=out_shape,
        scratch_shapes=[
            pltpu.VMEM((total, width), BF16),
            pltpu.VMEM((rows, width), BF16),
            pltpu.VMEM((2, total, width), BF16),
        ],
        compiler_params=pltpu.CompilerParams(vmem_limit_bytes=VMEM_LIMIT),
        cost_estimate=pl.CostEstimate(
            flops=2 * rows * total * width * 8, bytes_accessed=20 << 20, transcendentals=rows * total * 8
        ),
        name="cross_forward" if cross else "self_forward",
    )(scalars, *([rows_in] if cross else []), *all_in, project, biases, wo, gains, shifts)


def backward_body(cross, *refs):
    if cross:
        upstream_in, *refs = refs
    else:
        base_in, query_two, wq, *refs = refs
    normal, spread, gains, inverse, wo, mixed, query, keys, values, weights = refs[:10]
    out_query, out_key, out_value, out_small, out_rows, mixed_grad = refs[-6:]
    step = pl.program_id(0)
    rows, width = mixed.shape
    total = keys.shape[0]
    pair = pair_of(step)

    @pl.when(step == 0)
    def _():
        out_small[...] = jnp.zeros(out_small.shape, F32)
        if cross:
            upstream = upstream_in[...]
        else:
            upstream = base_in[...] + right_product(query_two[...], wq[0])
        normal_now = normal[...]
        grad = norm_backward(upstream, normal_now, spread[:, 0:1], wide_row(gains, 1 if cross else 0))
        out_small[0:1, :] = column_sum(upstream * normal_now)
        out_small[1:2, :] = column_sum(upstream)
        out_small[2:3, :] = column_sum(grad)
        out_rows[...] = grad
        mixed_grad[...] = (right_product(grad.astype(BF16), wo[...]) * inverse[...].astype(F32)).astype(BF16)

    keys_now, values_now = keys[...], values[...]
    key_grad = jnp.zeros((LANES, total), F32)
    value_grad = jnp.zeros((LANES, total), F32)
    query_grads = []
    for start in range(0, rows, CHUNK):
        span = slice(start, start + CHUNK)
        piece = query[span, :]
        grad = mixed_grad[span, pair]
        center = grad.astype(F32) * mixed[span, pair].astype(F32)
        found = []
        for head in range(2):
            grad_now = head_only(grad, head)
            center_now = jnp.sum(head_only(center, head), 1, keepdims=True)
            weight = weights[head, span, :]
            slope = right_product(grad_now, values_now)
            score_grad = (weight.astype(F32) * (slope - center_now)).astype(BF16)
            found.append(product(score_grad, keys_now))
            value_grad = value_grad + left_product(grad_now, weight)
            key_grad = key_grad + left_product(head_only(piece, head), score_grad)
        query_grads.append(head_pick(found[0], found[1]) * 0.125)
    query_grad = jnp.concatenate(query_grads, 0)
    value_grad = value_grad.T
    out_small[3:4, pair] = column_sum(query_grad)
    out_small[4:5, pair] = column_sum(value_grad)
    out_query[...] = query_grad.astype(BF16)
    out_key[...] = key_grad.T.astype(BF16)
    out_value[...] = value_grad.astype(BF16)


def attention_backward(cross, first_inputs, mixed, query, keys, values, weights, later=()):
    rows, width = mixed.shape
    total = keys.shape[0]
    pairs = width // LANES
    part = lambda count: pl.BlockSpec((count, LANES), lambda i: (0, i))
    front = [whole(1, *value.shape[1:]) if value.ndim == 3 else whole(*value.shape) for value in first_inputs]
    return pl.pallas_call(
        functools.partial(backward_body, cross),
        grid=(pairs,),
        in_specs=front
        + [whole(rows, width), part(rows), part(total), part(total)]
        + [pl.BlockSpec((2, rows, total), lambda i: (i, 0, 0))]
        + [LATER] * len(later),
        out_specs=[part(rows), part(total), part(total), whole(8, width), whole(rows, width)],
        out_shape=[
            jax.ShapeDtypeStruct((rows, width), BF16),
            jax.ShapeDtypeStruct((total, width), BF16),
            jax.ShapeDtypeStruct((total, width), BF16),
            jax.ShapeDtypeStruct((8, width), F32),
            jax.ShapeDtypeStruct((rows, width), F32),
        ],
        scratch_shapes=[pltpu.VMEM((rows, width), BF16)],
        compiler_params=pltpu.CompilerParams(vmem_limit_bytes=VMEM_LIMIT),
        cost_estimate=pl.CostEstimate(
            flops=2 * rows * total * width * 16, bytes_accessed=20 << 20, transcendentals=0
        ),
        name="cross_backward" if cross else "self_backward",
    )(*first_inputs, mixed, query, keys, values, weights, *later)


def weights_body(cross, scalars, *refs):
    ins, refs = refs[:11], refs[11:]
    if cross:
        slots, refs = refs[:2], refs[2:]
    else:
        smalls, refs = refs[:3], refs[3:]
    refs = refs[-18:]
    out_keep, out_send, out_own, out_other = refs[:4]
    mixed, grad_in, rows_in, every, query_in, key_in, value_in, project, grads, own, other, sem_in, sem_out = refs[4:17]
    rows, width = mixed.shape
    block = rows // 2
    even = lax.rem(scalars[0], 2) == 0
    here = [mixed, grad_in, rows_in, *[every.at[pl.ds(i * block, block)] for i in range(len(BLOCKS))],
            query_in, key_in, value_in, project]
    wanted = [0, 1, 2, 7, 3, 4, 5, 6, 8, 9, 10] if cross else [0, 1, 3, 4, 7, 5, 6, 8, 9, 10]
    coming = {i: pltpu.make_async_copy(ins[i], here[i], sem_in.at[i]) for i in wanted}
    for i in wanted:
        coming[i].start()

    def arrive(*which):
        for i in which:
            coming[i].wait()

    def span(index, count):
        return pl.ds(index * width, count)

    def leave(kept_by_even, index, value, number):
        count = value.shape[0]

        @pl.when(even if kept_by_even else jnp.logical_not(even))
        def _():
            pltpu.make_async_copy(value, out_keep.at[span(index, count)], sem_out.at[number]).start()

        @pl.when(jnp.logical_not(even) if kept_by_even else even)
        def _():
            pltpu.make_async_copy(value, out_send.at[span(index, count)], sem_out.at[number]).start()

    going = [pltpu.make_async_copy(grads.at[i], out_keep.at[span(i % 2, width)], sem_out.at[i]) for i in range(4)]
    if cross:
        extra = refs[17]
        slot_in = [pltpu.make_async_copy(slots[i], extra.at[i], sem_in.at[11 + i]) for i in range(2)]
        for i, out in enumerate((out_keep, out_send)):
            going.append(pltpu.make_async_copy(extra.at[i], out.at[span(2, width)], sem_out.at[4 + i]))
            slot_in[i].start()
    else:
        extra = refs[17]
        extra[0] = jnp.concatenate([ref[...] for ref in smalls] + [jnp.zeros((SMALL - 24, width), F32)], 0).astype(BF16)
        extra[1] = jnp.zeros((SMALL, width), BF16)
        for i in range(2):
            going.append(pltpu.make_async_copy(extra.at[i], out_keep.at[span(2, SMALL)], sem_out.at[4 + i]))
            leave(i == 0, 2, extra.at[i], 4 + i)

    arrive(0, 1)
    grads[0] = left_product(mixed[...], grad_in[...].astype(BF16)).astype(BF16)
    leave(True, 0, grads.at[0], 0)
    if cross:
        for i in range(2):
            slot_in[i].wait()
            going[4 + i].start()
        arrive(2, 7)
        grads[1] = left_product(rows_in[...], query_in[...]).astype(BF16)
    else:
        arrive(3, 4, 7)
        grads[1] = left_product(every[:rows, :], query_in[...]).astype(BF16)
    leave(True, 1, grads.at[1], 1)
    if cross:
        arrive(3, 4, 5, 6, 8)
    else:
        arrive(5, 6, 8)
    grads[2] = left_product(every[...], key_in[...]).astype(BF16)
    leave(False, 0, grads.at[2], 2)
    arrive(9)
    grads[3] = left_product(every[...], value_in[...]).astype(BF16)
    leave(False, 1, grads.at[3], 3)
    arrive(10)

    def onward(part):
        return right_product(key_in[part, :], project[1]) + right_product(value_in[part, :], project[2])

    other[...] = onward(slice(rows, 2 * rows)).astype(BF16)
    going.append(pltpu.make_async_copy(other, out_other, sem_out.at[6]))
    going[-1].start()
    value = onward(slice(0, rows))
    if not cross:
        value = value + grad_in[...] + right_product(query_in[...], project[0])
    own[...] = value
    going.append(pltpu.make_async_copy(own, out_own, sem_out.at[7]))
    going[-1].start()
    for copy in going:
        copy.wait()


VMEM = pl.BlockSpec(memory_space=pltpu.VMEM)


def weight_gradients(cross, scalars, mixed, grad, rows_in, all_in, grads, project, slots=(), later=()):
    block, width = all_in[0].shape
    rows, total = 2 * block, len(BLOCKS) * block
    count = 3 * width if cross else 2 * width + SMALL
    scratch = [
        pltpu.VMEM((rows, width), BF16),
        pltpu.VMEM((rows, width), F32),
        pltpu.VMEM((rows, width), BF16),
        pltpu.VMEM((total, width), BF16),
        pltpu.VMEM((rows, width), BF16),
        pltpu.VMEM((total, width), BF16),
        pltpu.VMEM((total, width), BF16),
        pltpu.VMEM((3, width, width), BF16),
        pltpu.VMEM((4, width, width), BF16),
        pltpu.VMEM((rows, width), F32),
        pltpu.VMEM((total - rows, width), BF16),
        pltpu.SemaphoreType.DMA((13,)),
        pltpu.SemaphoreType.DMA((8,)),
    ]
    scratch.append(pltpu.VMEM((2, width if cross else SMALL, width), BF16))
    return pl.pallas_call(
        functools.partial(weights_body, cross),
        in_specs=[SMEM] + [LATER] * 11 + [LATER if cross else VMEM] * len(slots) + [LATER] * len(later),
        out_specs=[LATER] * 4,
        out_shape=[
            jax.ShapeDtypeStruct((count, width), BF16),
            jax.ShapeDtypeStruct((count, width), BF16),
            jax.ShapeDtypeStruct((rows, width), F32),
            jax.ShapeDtypeStruct((total - rows, width), BF16),
        ],
        scratch_shapes=scratch,
        compiler_params=pltpu.CompilerParams(vmem_limit_bytes=VMEM_LIMIT),
        cost_estimate=pl.CostEstimate(flops=24 * rows * width * width, bytes_accessed=12 << 20, transcendentals=0),
        name="cross_weights" if cross else "self_weights",
    )(scalars, mixed, grad, rows_in, *all_in, *grads, project, *slots, *later)


SPLIT = 2


def gelu(value):
    square = value * value
    bent = jnp.tanh(0.7978845608028654 * value * (1.0 + 0.044715 * square))
    half = 0.5 * (1.0 + bent)
    slope = half + 0.5 * value * (1.0 - bent * bent) * (0.7978845608028654 + 3 * 0.044715 * 0.7978845608028654 * square)
    return value * half, slope


def feed_body(scalars, normal_two, gains, shifts, cot_one, cot_two, halo, wi, bi, wo, bo, slot_weight,
              out_keep, out_send, out_slot_keep, out_slot_send, out_state, out_grad, out_small,
              low, slopes, active, acc, low_grad):
    step = pl.program_id(0)
    rows, width = normal_two.shape
    block = rows // 2
    span = wi.shape[1]
    seat, size = scalars[0], scalars[1]
    even = lax.rem(seat, 2) == 0

    def store(kept_by_even, keep, send, index, value):
        value = value.astype(BF16)

        @pl.when(even if kept_by_even else jnp.logical_not(even))
        def _():
            keep[index] = value

        @pl.when(jnp.logical_not(even) if kept_by_even else even)
        def _():
            send[index] = value

    @pl.when(step == 0)
    def _():
        value = normal_two[...] * wide_row(gains, 1) + wide_row(shifts, 1)
        low[...] = value.astype(BF16)
        acc[...] = value + bo[...].astype(F32)

    @pl.when(step < SPLIT)
    def _():
        start = step * span
        value = product(low[...], wi[...]) + bi[...].astype(F32)
        found, slope = gelu(value)
        place = pl.ds(pl.multiple_of(start, span), span)
        slopes[:, place] = slope
        active[:, place] = found.astype(BF16)
        acc[...] += product(active[:, place], wo[...])

    @pl.when(step == SPLIT)
    def _():
        normal, inverse = norm_forward(acc[...])
        state = (normal * wide_row(gains, 2) + wide_row(shifts, 2)).astype(BF16)
        out_state[...] = state
        out_small[...] = jnp.zeros(out_small.shape, F32)
        place = lax.broadcasted_iota(jnp.int32, (block, 1), 0)
        sides = []
        for index, (item, cot) in enumerate(zip(BLOCKS[:2], (cot_one, cot_two))):
            first = (seat ^ item) * block
            value = cot[...].astype(F32)
            straight = jnp.where(first + place + 1 < size, value, 0.0)
            before = jnp.where(even, wide_row(halo, 1 - index), wide_row(halo, index))
            moved = jnp.where(place == 0, before, pltpu.roll(value, 1, 0))
            moved = jnp.where((first + place < size) & (first + place > 0), moved, 0.0)
            sides.append(jnp.concatenate([straight, moved], 1))
        sides = jnp.concatenate(sides, 0)
        out_small[0:1, :] = column_sum(sides[:, :width])
        sides = sides.astype(BF16)
        slot_grad = left_product(state, sides)
        store(True, out_slot_keep, out_slot_send, slice(None), slot_grad[:, :width])
        store(False, out_slot_keep, out_slot_send, slice(None), slot_grad[:, width:])
        state_grad = right_product(
            sides, jnp.concatenate([slot_weight[:width, :], slot_weight[width:, :]], 1)
        )
        out_small[1:2, :] = column_sum(state_grad * normal)
        out_small[2:3, :] = column_sum(state_grad)
        grad = norm_backward(state_grad, normal, inverse, wide_row(gains, 2))
        out_small[3:4, :] = column_sum(grad)
        acc[...] = grad
        low_grad[...] = grad.astype(BF16)

    @pl.when(step > SPLIT)
    def _():
        start = (step - SPLIT - 1) * span
        place = pl.ds(pl.multiple_of(start, span), span)
        grad = right_product(low_grad[...], wo[...]) * slopes[:, place]
        sums = column_sum(grad)
        first = 4 + (step - SPLIT - 1) * (span // width)
        for part in range(0, span, width):
            out_small[pl.ds(first + part // width, 1), :] = sums[:, part : part + width]
        grad_low = grad.astype(BF16)
        outer = left_product(active[:, place], low_grad[...])
        inner = left_product(low[...], grad_low)
        for part in range(0, span, width):
            store(True, out_keep, out_send, part // width, outer[part : part + width, :])
            store(False, out_keep, out_send, part // width, inner[:, part : part + width])
        acc[...] += right_product(grad_low, wi[...])

    @pl.when(step == pl.num_programs(0) - 1)
    def _():
        out_grad[...] = acc[...]


def feed_forward(scalars, normal_two, gains, shifts, cots, halo, wi, bi, wo, bo, slot_weight):
    rows, width = normal_two.shape
    hidden = wi.shape[1]
    span = hidden // SPLIT
    part = lambda i: jnp.where(i < SPLIT, i, jnp.maximum(i - SPLIT - 1, 0))
    group = pl.BlockSpec((span // width, width, width), lambda i: (jnp.maximum(i - SPLIT - 1, 0), 0, 0))
    grads = jax.ShapeDtypeStruct((hidden // width, width, width), BF16)
    slot = jax.ShapeDtypeStruct((width, width), BF16)
    return pl.pallas_call(
        feed_body,
        grid=(2 * SPLIT + 1,),
        in_specs=[
            SMEM,
            whole(rows, width),
            whole(3, width),
            whole(3, width),
            whole(rows // 2, width),
            whole(rows // 2, width),
            whole(2, width),
            pl.BlockSpec((width, span), lambda i: (0, part(i))),
            pl.BlockSpec((1, span), lambda i: (0, part(i))),
            pl.BlockSpec((span, width), lambda i: (part(i), 0)),
            whole(1, width),
            whole(2 * width, width),
        ],
        out_specs=[group, group, whole(width, width), whole(width, width), whole(rows, width), whole(rows, width),
                   whole(8, width)],
        out_shape=[
            grads,
            grads,
            slot,
            slot,
            jax.ShapeDtypeStruct((rows, width), BF16),
            jax.ShapeDtypeStruct((rows, width), F32),
            jax.ShapeDtypeStruct((8, width), F32),
        ],
        scratch_shapes=[
            pltpu.VMEM((rows, width), BF16),
            pltpu.VMEM((rows, hidden), F32),
            pltpu.VMEM((rows, hidden), BF16),
            pltpu.VMEM((rows, width), F32),
            pltpu.VMEM((rows, width), BF16),
        ],
        compiler_params=pltpu.CompilerParams(vmem_limit_bytes=VMEM_LIMIT),
        cost_estimate=pl.CostEstimate(
            flops=2 * rows * width * width * 32, bytes_accessed=20 << 20, transcendentals=rows * width * 8
        ),
        name="feed_forward",
    )(scalars, normal_two, gains, shifts, *cots, halo, wi, bi, wo, bo, slot_weight)


def slot_body(scalars, state, halo, slot_weight, slot_bias, out):
    rows, width = state.shape
    block = rows // 2
    seat, size = scalars[0], scalars[1]
    even = lax.rem(seat, 2) == 0
    place = lax.broadcasted_iota(jnp.int32, (block, 1), 0)
    for index, item in enumerate(BLOCKS[:2]):
        span = slice(index * block, (index + 1) * block)
        value = state[span, :]
        after = jnp.where(even, wide_row(halo, index), wide_row(halo, 1 - index))
        moved = jnp.where(place == block - 1, after, pltpu.roll(value.astype(F32), block - 1, 0)).astype(BF16)
        result = product(value, slot_weight[:width, :]) + product(moved, slot_weight[width:, :])
        result = result + slot_bias[...].astype(F32)
        out[span, :] = jnp.where((seat ^ item) * block + place + 1 < size, result, 0.0).astype(BF16)


def slot_states(scalars, state, halo, slot_weight, slot_bias):
    rows, width = state.shape
    vmem = pl.BlockSpec(memory_space=pltpu.VMEM)
    return pl.pallas_call(
        slot_body,
        in_specs=[SMEM] + [vmem] * 4,
        out_specs=vmem,
        out_shape=jax.ShapeDtypeStruct((rows, width), BF16),
        compiler_params=pltpu.CompilerParams(vmem_limit_bytes=16 << 20),
        cost_estimate=pl.CostEstimate(flops=4 * rows * width * width, bytes_accessed=4 << 20, transcendentals=0),
        name="slot_states",
    )(scalars, state, halo, slot_weight, slot_bias.reshape(1, -1))


def finish_body(hidden_parts, scalars, *refs):
    halves, refs = refs[:6], refs[6:]
    (out_outer, out_inner, out_cross_output, out_cross_project, out_slot, out_self_output, out_self_project,
     out_self, out_cross, out_gain, out_shift, out_inner_bias, out_outer_bias, out_slot_bias,
     feed, cross, own, wide, sem_in, sem_out) = refs
    width = feed.shape[2]
    odd = lax.rem(scalars[0], 2)
    groups = (feed, cross, own)
    coming = [
        [pltpu.make_async_copy(halves[2 * i + j], group.at[j], sem_in.at[2 * i + j]) for j in range(2)]
        for i, group in enumerate(groups)
    ]
    for pair in coming:
        for copy in pair:
            copy.start()
    rows = lambda index: pl.ds(index * width, width)
    targets = [
        [(i, 0, out_outer.at[rows(i)]) for i in range(hidden_parts)]
        + [(i, 1, out_inner.at[:, rows(i)]) for i in range(hidden_parts)],
        [(0, 0, out_cross_output), (1, 0, out_cross_project.at[0]), (2, 0, out_slot.at[rows(0)]),
         (0, 1, out_cross_project.at[1]), (1, 1, out_cross_project.at[2]), (2, 1, out_slot.at[rows(1)])],
        [(0, 0, out_self_output), (1, 0, out_self_project.at[0]),
         (0, 1, out_self_project.at[1]), (1, 1, out_self_project.at[2])],
    ]
    going = []
    for pair, group, places in zip(coming, groups, targets):
        for copy in pair:
            copy.wait()
        for chunk, side, out in places:
            number = len(going)
            source = odd if side == 0 else 1 - odd
            wide[number] = group[source, rows(chunk), :].astype(F32)
            going.append(pltpu.make_async_copy(wide.at[number], out, sem_out.at[number]))
            going[-1].start()
    small = own[odd, pl.ds(2 * width, 32), :].astype(F32)
    pick = lambda *places: jnp.concatenate([small[place : place + 1, :] for place in places], 0)
    out_self[...] = pick(19, 20, 18)
    out_cross[...] = pick(11, 12, 10)
    out_gain[...] = pick(16, 8, 1)
    out_shift[...] = pick(17, 9, 2)
    out_inner_bias[...] = jnp.concatenate([small[4 + i : 5 + i, :] for i in range(hidden_parts)], 1)
    out_outer_bias[...] = pick(3)
    out_slot_bias[...] = pick(0)
    for copy in going:
        copy.wait()


def finish(scalars, feed, cross, own, hidden):
    width = feed[0].shape[-1]
    parts = hidden // width
    feed = [value.reshape(-1, width) for value in feed]
    count = 2 * parts + 10
    shape = lambda *dims: jax.ShapeDtypeStruct(dims, F32)
    return pl.pallas_call(
        functools.partial(finish_body, parts),
        in_specs=[SMEM] + [LATER] * 6,
        out_specs=[LATER] * 7 + [VMEM] * 7,
        out_shape=[
            shape(hidden, width),
            shape(width, hidden),
            shape(width, width),
            shape(3, width, width),
            shape(2 * width, width),
            shape(width, width),
            shape(3, width, width),
            *[shape(3, width)] * 4,
            shape(1, hidden),
            shape(1, width),
            shape(1, width),
        ],
        scratch_shapes=[pltpu.VMEM((2, *value[0].shape), BF16) for value in (feed, cross, own)]
        + [pltpu.VMEM((count, width, width), F32), pltpu.SemaphoreType.DMA((6,)), pltpu.SemaphoreType.DMA((count,))],
        compiler_params=pltpu.CompilerParams(vmem_limit_bytes=VMEM_LIMIT),
        cost_estimate=pl.CostEstimate(flops=0, bytes_accessed=28 << 20, transcendentals=0),
        name="finish",
    )(scalars, *feed, *cross, *own)


def gate(values, after):
    count = len(values)
    return pl.pallas_call(
        lambda *refs: None,
        in_specs=[LATER] * (count + len(after)),
        out_specs=[LATER] * count,
        out_shape=[jax.ShapeDtypeStruct(value.shape, value.dtype) for value in values],
        input_output_aliases={index: index for index in range(count)},
        name="gate",
    )(*values, *after)


def swap(value, axis, bit):
    count = lax.axis_size(axis)
    return lax.ppermute(value, axis, [(place, place ^ bit) for place in range(count)])


def bit_of(axis, bit):
    return (lax.axis_index(axis) // bit) % 2


def routes():
    across, along = ("dp", 1), ("seq", 2)
    return [(across, along), (along, across)]


def rest_of_dp():
    rest, bit = [], 2
    while bit < lax.axis_size("dp"):
        rest.append(("dp", bit))
        bit *= 2
    return rest


def mixed_swap(value, step):
    if step[0] == step[1]:
        return swap(value, *step[0])
    groups, seats = lax.axis_size("dp"), lax.axis_size("seq")
    pairs = []
    for group in range(groups):
        for seat in range(seats):
            axis, bit = step[seat % 2]
            target = (group ^ bit, seat) if axis == "dp" else (group, seat ^ bit)
            pairs.append((group * seats + seat, target[0] * seats + target[1]))
    return lax.ppermute(value, ("dp", "seq"), pairs)


def mixed_bit(step):
    if step[0] == step[1]:
        return bit_of(*step[0])
    return jnp.where(lax.axis_index("seq") % 2 == 0, bit_of(*step[0]), bit_of(*step[1]))


class Sum:
    def __init__(self, keep, got):
        self.shape = keep.shape
        self.terms = [keep.reshape(-1, keep.shape[-1]), got.reshape(-1, keep.shape[-1])]
        self.steps = routes()
        self.rests = rest_of_dp()
        self.stage = 0
        self.last = 2 * len(self.steps) + len(self.rests)

    def halve(self, index, after=()):
        step = self.steps[index]
        half = self.terms[0].shape[0] // 2
        mine = mixed_bit(step) * half
        cut = lambda start: sum(lax.dynamic_slice_in_dim(term, start, half, 0) for term in self.terms)
        sent = cut(half - mine)
        if after:
            (sent,) = gate([sent], after)
        self.terms = [cut(mine), mixed_swap(sent, step)]
        return sent

    def add(self, step):
        value = sum(self.terms)
        self.terms = [value, swap(value, *step)]
        return value

    def double(self, index):
        step = self.steps[index]
        value = sum(self.terms)
        got = mixed_swap(value, step)
        lower = mixed_bit(step) == 0
        self.terms = [jnp.where(lower, jnp.concatenate([value, got], 0), jnp.concatenate([got, value], 0))]
        return value

    def finish(self):
        mine = self.terms[0].reshape(self.shape)
        return mine, swap(mine, "seq", 1)

    def next(self, *wait):
        if wait:
            self.terms = list(lax.optimization_barrier((*self.terms, *wait))[: len(self.terms)])
        count, place = len(self.steps), self.stage
        self.stage += 1
        if place < count:
            return self.halve(place)
        if place < count + len(self.rests):
            return self.add(self.rests[place - count])
        return self.double(self.last - 1 - place)

    def rest(self):
        while self.stage < self.last:
            self.next()
        return self.finish()


def per_device(
    canvas,
    memory,
    canvas_len,
    memory_len,
    slot_cot,
    self_project,
    self_output,
    self_biases,
    cross_project,
    cross_output,
    cross_biases,
    norm_gains,
    norm_shifts,
    inner_weight,
    inner_bias,
    outer_weight,
    outer_bias,
    slot_weight,
    slot_bias,
):
    block, width = canvas.shape[2:]
    seat = lax.axis_index("seq")
    batch = seat // 2
    upper = batch == 1

    def own_of(value, index):
        return lax.dynamic_index_in_dim(value, index, 0, keepdims=False)

    def placed(kept, got):
        got = got.astype(kept.dtype)
        return jnp.where(upper, jnp.stack([got, kept]), jnp.stack([kept, got]))[:, None]

    kept, away = own_of(canvas, batch)[0], own_of(canvas, 1 - batch)[0]
    scalars = jnp.stack(
        [seat.astype(jnp.int32), own_of(canvas_len, batch)[0], own_of(memory_len, batch)[0]]
    )
    inner_row, outer_row = inner_bias.reshape(1, -1), outer_bias.reshape(1, -1)
    cot_kept, cot_away = own_of(slot_cot, batch)[0], own_of(slot_cot, 1 - batch)[0]
    got, scalars, inner_row, outer_row, cot_away, cot_kept = lax.optimization_barrier(
        (swap(away, "seq", 2), scalars, inner_row, outer_row, cot_away, cot_kept)
    )
    every = [kept, got, swap(kept, "seq", 1), swap(got, "seq", 1)]
    kept, away = own_of(memory, batch)[0], own_of(memory, 1 - batch)[0]
    source_every = [kept, swap(away, "seq", 2), swap(kept, "seq", 1), swap(away, "seq", 3)]
    cots = [cot_kept, swap(cot_away, "seq", 2)]

    q, k, v, p, o, inverse, normal_one, spread_one = attention_forward(
        False, scalars, None, every, self_project, self_biases, self_output, norm_gains, norm_shifts
    )
    low_one, q2, k2, v2, p2, o2, inverse2, normal_two, spread_two = attention_forward(
        True, scalars, normal_one, source_every, cross_project, cross_biases, cross_output, norm_gains, norm_shifts
    )
    cot_halo = jnp.stack([swap(cot_kept[block - 1], "seq", 1), swap(cot_away[block - 1], "seq", 3)])
    feed_keep, feed_send, slot_keep, slot_send, state, grad_two, small_feed = feed_forward(
        scalars, normal_two, norm_gains, norm_shifts, cots, cot_halo, inner_weight, inner_row,
        outer_weight, outer_row, slot_weight,
    )

    feed = Sum(feed_keep, swap(feed_send, "seq", 1))
    state_halo = swap(jnp.stack([state[0], state[block]]), "seq", 1)
    dq2, dk2, dv2, small_cross, grad_mid = attention_backward(
        True, [grad_two, normal_two, spread_two, norm_gains, inverse2, cross_output], o2, q2, k2, v2, p2
    )
    sent = feed.halve(0, [dq2])
    feed.stage = 1
    cross_keep, cross_send, memory_own, memory_other = weight_gradients(
        True, scalars, o2, grad_mid, low_one, source_every, [dq2, dk2, dv2], cross_project,
        slots=[slot_keep, slot_send], later=[sent]
    )
    cross = Sum(cross_keep, swap(cross_send, "seq", 1))
    dq, dk, dv, small_self, grad_first = attention_backward(
        False, [grad_mid, dq2, cross_project, normal_one, spread_one, norm_gains, inverse, self_output],
        o, q, k, v, p, later=[cross_send],
    )
    sent = feed.halve(1)
    feed.stage = 2
    self_keep, self_send, canvas_own, canvas_other = weight_gradients(
        False, scalars, o, grad_first, every[0], every, [dq, dk, dv], self_project,
        slots=[small_feed, small_cross, small_self], later=[sent]
    )
    own = Sum(self_keep, swap(self_send, "seq", 1))

    slots = slot_states(scalars, state, state_halo, slot_weight, slot_bias)
    memory_total = memory_own + swap(memory_other, "seq", 1).astype(F32)
    canvas_total = canvas_own + swap(canvas_other, "seq", 1).astype(F32)

    slots_out = placed(slots[:block], swap(slots[block:], "seq", 2))
    canvas_out = placed(canvas_total[:block], swap(canvas_total[block:].astype(BF16), "seq", 2))
    memory_out = placed(memory_total[:block], swap(memory_total[block:].astype(BF16), "seq", 2))
    c0 = cross.next()
    o0 = own.next()
    c1 = cross.next(o0)
    o1 = own.next(c1)
    f2 = feed.next()
    f3 = feed.next(c1)
    c2 = cross.next(o1)
    o2 = own.next(c2)
    c3 = cross.next(o2)
    feed.next(slots_out)
    cross.next(memory_out)
    own.next()
    own.next(canvas_out)
    (grad_outer, grad_inner, grad_cross_output, grad_cross_project, grad_slot, grad_self_output, grad_self_project,
     grad_self_biases, grad_cross_biases, grad_gains, grad_shifts, grad_inner_bias, grad_outer_bias,
     grad_slot_bias) = finish(scalars, feed.rest(), cross.rest(), own.rest(), inner_bias.shape[0])
    return (
        slots_out,
        canvas_out,
        memory_out,
        grad_self_project,
        grad_self_output,
        grad_self_biases,
        grad_cross_project,
        grad_cross_output,
        grad_cross_biases,
        grad_gains,
        grad_shifts,
        grad_inner,
        grad_inner_bias.reshape(-1),
        grad_outer,
        grad_outer_bias.reshape(-1),
        grad_slot,
        grad_slot_bias.reshape(-1),
    )


def solution(mesh):
    tokens = P(None, "dp", "seq", None)
    sizes = P(None, "dp")
    return jax.shard_map(
        per_device,
        mesh=mesh,
        in_specs=(tokens, tokens, sizes, sizes, tokens) + (P(),) * 14,
        out_specs=(tokens,) * 3 + (P(),) * 14,
        check_vma=False,
    )
```

```python
import functools

import jax
import jax.numpy as jnp
from jax import lax
from jax.experimental import pallas as pl
from jax.experimental.pallas import tpu as pltpu
from jax.sharding import PartitionSpec as P

LANES = 128
CHUNK = 128
BACK_CHUNK = 512
SMALL = 128
EPSILON = 1e-05
MASKED = -1e30
VMEM_LIMIT = 60 << 20
F32 = jnp.float32
BF16 = jnp.bfloat16
BLOCKS = (0, 2, 1, 3)


def product(left, right):
    return jnp.dot(left, right, preferred_element_type=F32)


def left_product(left, right):
    return lax.dot_general(left, right, (((0,), (0,)), ((), ())), preferred_element_type=F32)


def right_product(left, right):
    return lax.dot_general(left, right, (((1,), (1,)), ((), ())), preferred_element_type=F32)


def column_sum(value):
    return jnp.sum(value, 0, keepdims=True)


def norm_forward(value):
    mean = jnp.mean(value, -1, keepdims=True)
    centered = value - mean
    spread = jnp.mean(centered * centered, -1, keepdims=True)
    inverse = lax.rsqrt(spread + EPSILON)
    return centered * inverse, inverse


def norm_backward(upstream, normal, inverse, gain):
    scaled = upstream * gain
    inner_mean = jnp.mean(scaled, -1, keepdims=True)
    cross_mean = jnp.mean(scaled * normal, -1, keepdims=True)
    return inverse * (scaled - inner_mean - normal * cross_mean)


def wide_row(ref, row):
    return ref[row : row + 1, :].astype(F32)


def head_only(value, which):
    lane = lax.broadcasted_iota(jnp.int32, (1, LANES), 1)
    mine = lane < LANES // 2 if which == 0 else lane >= LANES // 2
    return jnp.where(mine, value, jnp.zeros_like(value))


def head_pick(first, second):
    lane = lax.broadcasted_iota(jnp.int32, (1, LANES), 1)
    return jnp.where(lane < LANES // 2, first, second)


def pair_of(step):
    return pl.ds(pl.multiple_of(step * LANES, LANES), LANES)


def forward_body(cross, scalars, *refs):
    if cross:
        rows_in, *refs = refs
    all_in, refs = refs[: len(BLOCKS)], refs[len(BLOCKS) :]
    project, biases, wo, gains, shifts, *refs = refs
    if cross:
        out_low, *refs = refs
    out_q, out_k, out_v, out_p, out_o, out_inverse, out_normal, out_spread = refs[:8]
    every, queries, both_all = refs[8:]
    step = pl.program_id(0)
    block = all_in[0].shape[0]
    width = every.shape[1]
    rows, total = 2 * block, len(BLOCKS) * block
    seat, size = scalars[0], scalars[2 if cross else 1]

    @pl.when(step == 0)
    def _():
        for index, ref in enumerate(all_in):
            every[index * block : (index + 1) * block, :] = ref[...]
        if cross:
            value = rows_in[...] * wide_row(gains, 0) + wide_row(shifts, 0)
            out_low[...] = value.astype(BF16)
            source = out_low[...]
        else:
            source = every[:rows, :]
        query = product(source, project[0]) + wide_row(biases, 0)
        queries[...] = query.astype(BF16) * jnp.asarray(0.125, BF16)
        both_all[0] = product(every[...], project[1]).astype(BF16)
        both_all[1] = (product(every[...], project[2]) + wide_row(biases, 1)).astype(BF16)

    query = queries[:, pair_of(step)]
    keys = both_all[0, :, pair_of(step)]
    values = both_all[1, :, pair_of(step)]
    out_q[...] = query
    out_k[...] = keys
    out_v[...] = values
    wide = jnp.concatenate([values, jnp.ones((total, LANES), BF16)], 1)
    place = lax.broadcasted_iota(jnp.int32, (1, block), 1)
    bias = jnp.concatenate(
        [jnp.where((seat ^ item) * block + place < size, 0.0, MASKED) for item in BLOCKS], 1
    )
    for start in range(0, rows, CHUNK):
        piece = query[start : start + CHUNK]
        parts = []
        for head in range(2):
            scores = right_product(head_only(piece, head), keys) + bias
            weights = jnp.exp(scores - jnp.max(scores, 1, keepdims=True)).astype(BF16)
            out_p[head, start : start + CHUNK, :] = weights
            result = product(weights, wide)
            inverse = 1.0 / result[:, LANES:]
            parts.append((result[:, :LANES] * inverse, inverse))
        out_o[start : start + CHUNK, pair_of(step)] = head_pick(parts[0][0], parts[1][0]).astype(BF16)
        out_inverse[start : start + CHUNK, pair_of(step)] = head_pick(parts[0][1], parts[1][1]).astype(BF16)

    @pl.when(step == pl.num_programs(0) - 1)
    def _():
        if cross:
            base = rows_in[...] * wide_row(gains, 0) + wide_row(shifts, 0)
        else:
            base = every[:rows, :].astype(F32)
        value = base + product(out_o[...], wo[...]) + wide_row(biases, 2)
        normal, inverse = norm_forward(value)
        out_normal[...] = normal
        out_spread[...] = jnp.broadcast_to(inverse, out_spread.shape)


def whole(*shape):
    return pl.BlockSpec(shape, lambda i: (0,) * len(shape))


SMEM = pl.BlockSpec(memory_space=pltpu.SMEM)
LATER = pl.BlockSpec(memory_space=pl.ANY)


def attention_forward(cross, scalars, rows_in, all_in, project, biases, wo, gains, shifts):
    block, width = all_in[0].shape
    rows, total = 2 * block, len(BLOCKS) * block
    pairs = width // LANES
    part = lambda count: pl.BlockSpec((count, LANES), lambda i: (0, i))
    out_shape = [
        jax.ShapeDtypeStruct((rows, width), BF16),
        jax.ShapeDtypeStruct((total, width), BF16),
        jax.ShapeDtypeStruct((total, width), BF16),
        jax.ShapeDtypeStruct((2 * pairs, rows, total), BF16),
        jax.ShapeDtypeStruct((rows, width), BF16),
        jax.ShapeDtypeStruct((rows, width), BF16),
        jax.ShapeDtypeStruct((rows, width), F32),
        jax.ShapeDtypeStruct((rows, LANES), F32),
    ]
    out_specs = [
        part(rows),
        part(total),
        part(total),
        pl.BlockSpec((2, rows, total), lambda i: (i, 0, 0)),
        whole(rows, width),
        whole(rows, width),
        whole(rows, width),
        whole(rows, LANES),
    ]
    if cross:
        out_shape = [jax.ShapeDtypeStruct((rows, width), BF16)] + out_shape
        out_specs = [whole(rows, width)] + out_specs
    return pl.pallas_call(
        functools.partial(forward_body, cross),
        grid=(pairs,),
        in_specs=[SMEM]
        + ([whole(rows, width)] if cross else [])
        + [whole(block, width)] * len(BLOCKS)
        + [whole(3, width, width), whole(3, width), whole(width, width), whole(3, width), whole(3, width)],
        out_specs=out_specs,
        out_shape=out_shape,
        scratch_shapes=[
            pltpu.VMEM((total, width), BF16),
            pltpu.VMEM((rows, width), BF16),
            pltpu.VMEM((2, total, width), BF16),
        ],
        compiler_params=pltpu.CompilerParams(vmem_limit_bytes=VMEM_LIMIT),
        cost_estimate=pl.CostEstimate(
            flops=2 * rows * total * width * 8, bytes_accessed=20 << 20, transcendentals=rows * total * 8
        ),
        name="cross_forward" if cross else "self_forward",
    )(scalars, *([rows_in] if cross else []), *all_in, project, biases, wo, gains, shifts)


def backward_body(cross, *refs):
    if cross:
        upstream_in, *refs = refs
    else:
        base_in, query_two, wq, *refs = refs
    normal, spread, gains, inverse, wo, mixed, query, keys, values, weights = refs[:10]
    out_query, out_key, out_value, out_small, out_rows, mixed_grad = refs[-6:]
    step = pl.program_id(0)
    rows, width = mixed.shape
    total = keys.shape[0]
    pair = pair_of(step)

    @pl.when(step == 0)
    def _():
        out_small[...] = jnp.zeros(out_small.shape, F32)
        if cross:
            upstream = upstream_in[...]
        else:
            upstream = base_in[...] + right_product(query_two[...], wq[0])
        normal_now = normal[...]
        grad = norm_backward(upstream, normal_now, spread[:, 0:1], wide_row(gains, 1 if cross else 0))
        out_small[0:1, :] = column_sum(upstream * normal_now)
        out_small[1:2, :] = column_sum(upstream)
        out_small[2:3, :] = column_sum(grad)
        out_rows[...] = grad
        mixed_grad[...] = (right_product(grad.astype(BF16), wo[...]) * inverse[...].astype(F32)).astype(BF16)

    keys_now, values_now = keys[...], values[...]
    key_grad = jnp.zeros((LANES, total), F32)
    value_grad = jnp.zeros((LANES, total), F32)
    query_grads = []
    for start in range(0, rows, BACK_CHUNK):
        span = slice(start, start + BACK_CHUNK)
        piece = query[span, :]
        grad = mixed_grad[span, pair]
        center = grad.astype(F32) * mixed[span, pair].astype(F32)
        found = []
        for head in range(2):
            grad_now = head_only(grad, head)
            center_now = jnp.sum(head_only(center, head), 1, keepdims=True)
            weight = weights[head, span, :]
            slope = right_product(grad_now, values_now)
            score_grad = (weight.astype(F32) * (slope - center_now)).astype(BF16)
            found.append(product(score_grad, keys_now))
            value_grad = value_grad + left_product(grad_now, weight)
            key_grad = key_grad + left_product(head_only(piece, head), score_grad)
        query_grads.append(head_pick(found[0], found[1]) * 0.125)
    query_grad = jnp.concatenate(query_grads, 0)
    value_grad = value_grad.T
    out_small[3:4, pair] = column_sum(query_grad)
    out_small[4:5, pair] = column_sum(value_grad)
    out_query[...] = query_grad.astype(BF16)
    out_key[...] = key_grad.T.astype(BF16)
    out_value[...] = value_grad.astype(BF16)


def attention_backward(cross, first_inputs, mixed, query, keys, values, weights, later=()):
    rows, width = mixed.shape
    total = keys.shape[0]
    pairs = width // LANES
    part = lambda count: pl.BlockSpec((count, LANES), lambda i: (0, i))
    front = [whole(1, *value.shape[1:]) if value.ndim == 3 else whole(*value.shape) for value in first_inputs]
    return pl.pallas_call(
        functools.partial(backward_body, cross),
        grid=(pairs,),
        in_specs=front
        + [whole(rows, width), part(rows), part(total), part(total)]
        + [pl.BlockSpec((2, rows, total), lambda i: (i, 0, 0))]
        + [LATER] * len(later),
        out_specs=[part(rows), part(total), part(total), whole(8, width), whole(rows, width)],
        out_shape=[
            jax.ShapeDtypeStruct((rows, width), BF16),
            jax.ShapeDtypeStruct((total, width), BF16),
            jax.ShapeDtypeStruct((total, width), BF16),
            jax.ShapeDtypeStruct((8, width), F32),
            jax.ShapeDtypeStruct((rows, width), F32),
        ],
        scratch_shapes=[pltpu.VMEM((rows, width), BF16)],
        compiler_params=pltpu.CompilerParams(vmem_limit_bytes=VMEM_LIMIT),
        cost_estimate=pl.CostEstimate(
            flops=2 * rows * total * width * 16, bytes_accessed=20 << 20, transcendentals=0
        ),
        name="cross_backward" if cross else "self_backward",
    )(*first_inputs, mixed, query, keys, values, weights, *later)


def weights_body(cross, scalars, *refs):
    ins, refs = refs[:11], refs[11:]
    if cross:
        slots, refs = refs[:2], refs[2:]
    else:
        smalls, refs = refs[:3], refs[3:]
    refs = refs[-18:]
    out_keep, out_send, out_own, out_other = refs[:4]
    mixed, grad_in, rows_in, every, query_in, key_in, value_in, project, grads, own, other, sem_in, sem_out = refs[4:17]
    rows, width = mixed.shape
    block = rows // 2
    even = lax.rem(scalars[0], 2) == 0
    here = [mixed, grad_in, rows_in, *[every.at[pl.ds(i * block, block)] for i in range(len(BLOCKS))],
            query_in, key_in, value_in, project]
    wanted = [0, 1, 2, 7, 3, 4, 5, 6, 8, 9, 10] if cross else [0, 1, 3, 4, 7, 5, 6, 8, 9, 10]
    coming = {i: pltpu.make_async_copy(ins[i], here[i], sem_in.at[i]) for i in wanted}
    for i in wanted:
        coming[i].start()

    def arrive(*which):
        for i in which:
            coming[i].wait()

    def span(index, count):
        return pl.ds(index * width, count)

    def leave(kept_by_even, index, value, number):
        count = value.shape[0]

        @pl.when(even if kept_by_even else jnp.logical_not(even))
        def _():
            pltpu.make_async_copy(value, out_keep.at[span(index, count)], sem_out.at[number]).start()

        @pl.when(jnp.logical_not(even) if kept_by_even else even)
        def _():
            pltpu.make_async_copy(value, out_send.at[span(index, count)], sem_out.at[number]).start()

    going = [pltpu.make_async_copy(grads.at[i], out_keep.at[span(i % 2, width)], sem_out.at[i]) for i in range(4)]
    if cross:
        extra = refs[17]
        slot_in = [pltpu.make_async_copy(slots[i], extra.at[i], sem_in.at[11 + i]) for i in range(2)]
        for i, out in enumerate((out_keep, out_send)):
            going.append(pltpu.make_async_copy(extra.at[i], out.at[span(2, width)], sem_out.at[4 + i]))
            slot_in[i].start()
    else:
        extra = refs[17]
        extra[0] = jnp.concatenate([ref[...] for ref in smalls] + [jnp.zeros((SMALL - 24, width), F32)], 0).astype(BF16)
        extra[1] = jnp.zeros((SMALL, width), BF16)
        for i in range(2):
            going.append(pltpu.make_async_copy(extra.at[i], out_keep.at[span(2, SMALL)], sem_out.at[4 + i]))
            leave(i == 0, 2, extra.at[i], 4 + i)

    arrive(0, 1)
    grads[0] = left_product(mixed[...], grad_in[...].astype(BF16)).astype(BF16)
    leave(True, 0, grads.at[0], 0)
    if cross:
        for i in range(2):
            slot_in[i].wait()
            going[4 + i].start()
        arrive(2, 7)
        grads[1] = left_product(rows_in[...], query_in[...]).astype(BF16)
    else:
        arrive(3, 4, 7)
        grads[1] = left_product(every[:rows, :], query_in[...]).astype(BF16)
    leave(True, 1, grads.at[1], 1)
    if cross:
        arrive(3, 4, 5, 6, 8)
    else:
        arrive(5, 6, 8)
    grads[2] = left_product(every[...], key_in[...]).astype(BF16)
    leave(False, 0, grads.at[2], 2)
    arrive(9)
    grads[3] = left_product(every[...], value_in[...]).astype(BF16)
    leave(False, 1, grads.at[3], 3)
    arrive(10)

    def onward(part):
        return right_product(key_in[part, :], project[1]) + right_product(value_in[part, :], project[2])

    other[...] = onward(slice(rows, 2 * rows)).astype(BF16)
    going.append(pltpu.make_async_copy(other, out_other, sem_out.at[6]))
    going[-1].start()
    value = onward(slice(0, rows))
    if not cross:
        value = value + grad_in[...] + right_product(query_in[...], project[0])
    own[...] = value
    going.append(pltpu.make_async_copy(own, out_own, sem_out.at[7]))
    going[-1].start()
    for copy in going:
        copy.wait()


VMEM = pl.BlockSpec(memory_space=pltpu.VMEM)


def weight_gradients(cross, scalars, mixed, grad, rows_in, all_in, grads, project, slots=(), later=()):
    block, width = all_in[0].shape
    rows, total = 2 * block, len(BLOCKS) * block
    count = 3 * width if cross else 2 * width + SMALL
    scratch = [
        pltpu.VMEM((rows, width), BF16),
        pltpu.VMEM((rows, width), F32),
        pltpu.VMEM((rows, width), BF16),
        pltpu.VMEM((total, width), BF16),
        pltpu.VMEM((rows, width), BF16),
        pltpu.VMEM((total, width), BF16),
        pltpu.VMEM((total, width), BF16),
        pltpu.VMEM((3, width, width), BF16),
        pltpu.VMEM((4, width, width), BF16),
        pltpu.VMEM((rows, width), F32),
        pltpu.VMEM((total - rows, width), BF16),
        pltpu.SemaphoreType.DMA((13,)),
        pltpu.SemaphoreType.DMA((8,)),
    ]
    scratch.append(pltpu.VMEM((2, width if cross else SMALL, width), BF16))
    return pl.pallas_call(
        functools.partial(weights_body, cross),
        in_specs=[SMEM] + [LATER] * 11 + [LATER if cross else VMEM] * len(slots) + [LATER] * len(later),
        out_specs=[LATER] * 4,
        out_shape=[
            jax.ShapeDtypeStruct((count, width), BF16),
            jax.ShapeDtypeStruct((count, width), BF16),
            jax.ShapeDtypeStruct((rows, width), F32),
            jax.ShapeDtypeStruct((total - rows, width), BF16),
        ],
        scratch_shapes=scratch,
        compiler_params=pltpu.CompilerParams(vmem_limit_bytes=VMEM_LIMIT),
        cost_estimate=pl.CostEstimate(flops=24 * rows * width * width, bytes_accessed=12 << 20, transcendentals=0),
        name="cross_weights" if cross else "self_weights",
    )(scalars, mixed, grad, rows_in, *all_in, *grads, project, *slots, *later)


SPLIT = 2


def gelu(value):
    square = value * value
    bent = jnp.tanh(0.7978845608028654 * value * (1.0 + 0.044715 * square))
    half = 0.5 * (1.0 + bent)
    slope = half + 0.5 * value * (1.0 - bent * bent) * (0.7978845608028654 + 3 * 0.044715 * 0.7978845608028654 * square)
    return value * half, slope


def feed_body(scalars, normal_two, gains, shifts, cot_one, cot_two, halo, wi, bi, wo, bo, slot_weight,
              out_keep, out_send, out_slot_keep, out_slot_send, out_state, out_grad, out_small,
              low, slopes, active, acc, low_grad):
    step = pl.program_id(0)
    rows, width = normal_two.shape
    block = rows // 2
    span = wi.shape[1]
    seat, size = scalars[0], scalars[1]
    even = lax.rem(seat, 2) == 0

    def store(kept_by_even, keep, send, index, value):
        value = value.astype(BF16)

        @pl.when(even if kept_by_even else jnp.logical_not(even))
        def _():
            keep[index] = value

        @pl.when(jnp.logical_not(even) if kept_by_even else even)
        def _():
            send[index] = value

    @pl.when(step == 0)
    def _():
        value = normal_two[...] * wide_row(gains, 1) + wide_row(shifts, 1)
        low[...] = value.astype(BF16)
        acc[...] = value + bo[...].astype(F32)

    @pl.when(step < SPLIT)
    def _():
        start = step * span
        value = product(low[...], wi[...]) + bi[...].astype(F32)
        found, slope = gelu(value)
        place = pl.ds(pl.multiple_of(start, span), span)
        slopes[:, place] = slope
        active[:, place] = found.astype(BF16)
        acc[...] += product(active[:, place], wo[...])

    @pl.when(step == SPLIT)
    def _():
        normal, inverse = norm_forward(acc[...])
        state = (normal * wide_row(gains, 2) + wide_row(shifts, 2)).astype(BF16)
        out_state[...] = state
        out_small[...] = jnp.zeros(out_small.shape, F32)
        place = lax.broadcasted_iota(jnp.int32, (block, 1), 0)
        sides = []
        for index, (item, cot) in enumerate(zip(BLOCKS[:2], (cot_one, cot_two))):
            first = (seat ^ item) * block
            value = cot[...].astype(F32)
            straight = jnp.where(first + place + 1 < size, value, 0.0)
            before = jnp.where(even, wide_row(halo, 1 - index), wide_row(halo, index))
            moved = jnp.where(place == 0, before, pltpu.roll(value, 1, 0))
            moved = jnp.where((first + place < size) & (first + place > 0), moved, 0.0)
            sides.append(jnp.concatenate([straight, moved], 1))
        sides = jnp.concatenate(sides, 0)
        out_small[0:1, :] = column_sum(sides[:, :width])
        sides = sides.astype(BF16)
        slot_grad = left_product(state, sides)
        store(True, out_slot_keep, out_slot_send, slice(None), slot_grad[:, :width])
        store(False, out_slot_keep, out_slot_send, slice(None), slot_grad[:, width:])
        state_grad = right_product(
            sides, jnp.concatenate([slot_weight[:width, :], slot_weight[width:, :]], 1)
        )
        out_small[1:2, :] = column_sum(state_grad * normal)
        out_small[2:3, :] = column_sum(state_grad)
        grad = norm_backward(state_grad, normal, inverse, wide_row(gains, 2))
        out_small[3:4, :] = column_sum(grad)
        acc[...] = grad
        low_grad[...] = grad.astype(BF16)

    @pl.when(step > SPLIT)
    def _():
        start = (step - SPLIT - 1) * span
        place = pl.ds(pl.multiple_of(start, span), span)
        grad = right_product(low_grad[...], wo[...]) * slopes[:, place]
        sums = column_sum(grad)
        first = 4 + (step - SPLIT - 1) * (span // width)
        for part in range(0, span, width):
            out_small[pl.ds(first + part // width, 1), :] = sums[:, part : part + width]
        grad_low = grad.astype(BF16)
        outer = left_product(active[:, place], low_grad[...])
        inner = left_product(low[...], grad_low)
        for part in range(0, span, width):
            store(True, out_keep, out_send, part // width, outer[part : part + width, :])
            store(False, out_keep, out_send, part // width, inner[:, part : part + width])
        acc[...] += right_product(grad_low, wi[...])

    @pl.when(step == pl.num_programs(0) - 1)
    def _():
        out_grad[...] = acc[...]


def feed_forward(scalars, normal_two, gains, shifts, cots, halo, wi, bi, wo, bo, slot_weight):
    rows, width = normal_two.shape
    hidden = wi.shape[1]
    span = hidden // SPLIT
    part = lambda i: jnp.where(i < SPLIT, i, jnp.maximum(i - SPLIT - 1, 0))
    group = pl.BlockSpec((span // width, width, width), lambda i: (jnp.maximum(i - SPLIT - 1, 0), 0, 0))
    grads = jax.ShapeDtypeStruct((hidden // width, width, width), BF16)
    slot = jax.ShapeDtypeStruct((width, width), BF16)
    return pl.pallas_call(
        feed_body,
        grid=(2 * SPLIT + 1,),
        in_specs=[
            SMEM,
            whole(rows, width),
            whole(3, width),
            whole(3, width),
            whole(rows // 2, width),
            whole(rows // 2, width),
            whole(2, width),
            pl.BlockSpec((width, span), lambda i: (0, part(i))),
            pl.BlockSpec((1, span), lambda i: (0, part(i))),
            pl.BlockSpec((span, width), lambda i: (part(i), 0)),
            whole(1, width),
            whole(2 * width, width),
        ],
        out_specs=[group, group, whole(width, width), whole(width, width), whole(rows, width), whole(rows, width),
                   whole(8, width)],
        out_shape=[
            grads,
            grads,
            slot,
            slot,
            jax.ShapeDtypeStruct((rows, width), BF16),
            jax.ShapeDtypeStruct((rows, width), F32),
            jax.ShapeDtypeStruct((8, width), F32),
        ],
        scratch_shapes=[
            pltpu.VMEM((rows, width), BF16),
            pltpu.VMEM((rows, hidden), F32),
            pltpu.VMEM((rows, hidden), BF16),
            pltpu.VMEM((rows, width), F32),
            pltpu.VMEM((rows, width), BF16),
        ],
        compiler_params=pltpu.CompilerParams(vmem_limit_bytes=VMEM_LIMIT),
        cost_estimate=pl.CostEstimate(
            flops=2 * rows * width * width * 32, bytes_accessed=20 << 20, transcendentals=rows * width * 8
        ),
        name="feed_forward",
    )(scalars, normal_two, gains, shifts, *cots, halo, wi, bi, wo, bo, slot_weight)


def slot_body(scalars, state, halo, slot_weight, slot_bias, out):
    rows, width = state.shape
    block = rows // 2
    seat, size = scalars[0], scalars[1]
    even = lax.rem(seat, 2) == 0
    place = lax.broadcasted_iota(jnp.int32, (block, 1), 0)
    for index, item in enumerate(BLOCKS[:2]):
        span = slice(index * block, (index + 1) * block)
        value = state[span, :]
        after = jnp.where(even, wide_row(halo, index), wide_row(halo, 1 - index))
        moved = jnp.where(place == block - 1, after, pltpu.roll(value.astype(F32), block - 1, 0)).astype(BF16)
        result = product(value, slot_weight[:width, :]) + product(moved, slot_weight[width:, :])
        result = result + slot_bias[...].astype(F32)
        out[span, :] = jnp.where((seat ^ item) * block + place + 1 < size, result, 0.0).astype(BF16)


def slot_states(scalars, state, halo, slot_weight, slot_bias):
    rows, width = state.shape
    vmem = pl.BlockSpec(memory_space=pltpu.VMEM)
    return pl.pallas_call(
        slot_body,
        in_specs=[SMEM] + [vmem] * 4,
        out_specs=vmem,
        out_shape=jax.ShapeDtypeStruct((rows, width), BF16),
        compiler_params=pltpu.CompilerParams(vmem_limit_bytes=16 << 20),
        cost_estimate=pl.CostEstimate(flops=4 * rows * width * width, bytes_accessed=4 << 20, transcendentals=0),
        name="slot_states",
    )(scalars, state, halo, slot_weight, slot_bias.reshape(1, -1))


def finish_body(hidden_parts, scalars, *refs):
    halves, refs = refs[:6], refs[6:]
    (out_outer, out_inner, out_cross_output, out_cross_project, out_slot, out_self_output, out_self_project,
     out_self, out_cross, out_gain, out_shift, out_inner_bias, out_outer_bias, out_slot_bias,
     feed, cross, own, wide, sem_in, sem_out) = refs
    width = feed.shape[2]
    odd = lax.rem(scalars[0], 2)
    groups = (feed, cross, own)
    coming = [
        [pltpu.make_async_copy(halves[2 * i + j], group.at[j], sem_in.at[2 * i + j]) for j in range(2)]
        for i, group in enumerate(groups)
    ]
    for pair in coming:
        for copy in pair:
            copy.start()
    rows = lambda index: pl.ds(index * width, width)
    targets = [
        [(i, 0, out_outer.at[rows(i)]) for i in range(hidden_parts)]
        + [(i, 1, out_inner.at[:, rows(i)]) for i in range(hidden_parts)],
        [(0, 0, out_cross_output), (1, 0, out_cross_project.at[0]), (2, 0, out_slot.at[rows(0)]),
         (0, 1, out_cross_project.at[1]), (1, 1, out_cross_project.at[2]), (2, 1, out_slot.at[rows(1)])],
        [(0, 0, out_self_output), (1, 0, out_self_project.at[0]),
         (0, 1, out_self_project.at[1]), (1, 1, out_self_project.at[2])],
    ]
    going = []
    for pair, group, places in zip(coming, groups, targets):
        for copy in pair:
            copy.wait()
        for chunk, side, out in places:
            number = len(going)
            source = odd if side == 0 else 1 - odd
            wide[number] = group[source, rows(chunk), :].astype(F32)
            going.append(pltpu.make_async_copy(wide.at[number], out, sem_out.at[number]))
            going[-1].start()
    small = own[odd, pl.ds(2 * width, 32), :].astype(F32)
    pick = lambda *places: jnp.concatenate([small[place : place + 1, :] for place in places], 0)
    out_self[...] = pick(19, 20, 18)
    out_cross[...] = pick(11, 12, 10)
    out_gain[...] = pick(16, 8, 1)
    out_shift[...] = pick(17, 9, 2)
    out_inner_bias[...] = jnp.concatenate([small[4 + i : 5 + i, :] for i in range(hidden_parts)], 1)
    out_outer_bias[...] = pick(3)
    out_slot_bias[...] = pick(0)
    for copy in going:
        copy.wait()


def finish(scalars, feed, cross, own, hidden):
    width = feed[0].shape[-1]
    parts = hidden // width
    feed = [value.reshape(-1, width) for value in feed]
    count = 2 * parts + 10
    shape = lambda *dims: jax.ShapeDtypeStruct(dims, F32)
    return pl.pallas_call(
        functools.partial(finish_body, parts),
        in_specs=[SMEM] + [LATER] * 6,
        out_specs=[LATER] * 7 + [VMEM] * 7,
        out_shape=[
            shape(hidden, width),
            shape(width, hidden),
            shape(width, width),
            shape(3, width, width),
            shape(2 * width, width),
            shape(width, width),
            shape(3, width, width),
            *[shape(3, width)] * 4,
            shape(1, hidden),
            shape(1, width),
            shape(1, width),
        ],
        scratch_shapes=[pltpu.VMEM((2, *value[0].shape), BF16) for value in (feed, cross, own)]
        + [pltpu.VMEM((count, width, width), F32), pltpu.SemaphoreType.DMA((6,)), pltpu.SemaphoreType.DMA((count,))],
        compiler_params=pltpu.CompilerParams(vmem_limit_bytes=VMEM_LIMIT),
        cost_estimate=pl.CostEstimate(flops=0, bytes_accessed=28 << 20, transcendentals=0),
        name="finish",
    )(scalars, *feed, *cross, *own)


def gate(values, after):
    count = len(values)
    return pl.pallas_call(
        lambda *refs: None,
        in_specs=[LATER] * (count + len(after)),
        out_specs=[LATER] * count,
        out_shape=[jax.ShapeDtypeStruct(value.shape, value.dtype) for value in values],
        input_output_aliases={index: index for index in range(count)},
        name="gate",
    )(*values, *after)


def swap(value, axis, bit):
    count = lax.axis_size(axis)
    return lax.ppermute(value, axis, [(place, place ^ bit) for place in range(count)])


def bit_of(axis, bit):
    return (lax.axis_index(axis) // bit) % 2


def routes():
    across, along = ("dp", 1), ("seq", 2)
    return [(across, along), (along, across)]


def rest_of_dp():
    rest, bit = [], 2
    while bit < lax.axis_size("dp"):
        rest.append(("dp", bit))
        bit *= 2
    return rest


def mixed_swap(value, step):
    if step[0] == step[1]:
        return swap(value, *step[0])
    groups, seats = lax.axis_size("dp"), lax.axis_size("seq")
    pairs = []
    for group in range(groups):
        for seat in range(seats):
            axis, bit = step[seat % 2]
            target = (group ^ bit, seat) if axis == "dp" else (group, seat ^ bit)
            pairs.append((group * seats + seat, target[0] * seats + target[1]))
    return lax.ppermute(value, ("dp", "seq"), pairs)


def mixed_bit(step):
    if step[0] == step[1]:
        return bit_of(*step[0])
    return jnp.where(lax.axis_index("seq") % 2 == 0, bit_of(*step[0]), bit_of(*step[1]))


class Sum:
    def __init__(self, keep, got, depth):
        self.shape = keep.shape
        self.terms = [keep.reshape(-1, keep.shape[-1]), got.reshape(-1, keep.shape[-1])]
        rest = rest_of_dp()
        self.steps = routes() + [(step, step) for step in rest[:depth]]
        self.rests = rest[depth:]
        self.stage = 0
        self.last = 2 * len(self.steps) + len(self.rests)

    def halve(self, index, after=()):
        step = self.steps[index]
        half = self.terms[0].shape[0] // 2
        mine = mixed_bit(step) * half
        cut = lambda start: sum(lax.dynamic_slice_in_dim(term, start, half, 0) for term in self.terms)
        sent = cut(half - mine)
        if after:
            (sent,) = gate([sent], after)
        self.terms = [cut(mine), mixed_swap(sent, step)]
        return sent

    def add(self, step):
        value = sum(self.terms)
        self.terms = [value, swap(value, *step)]
        return value

    def double(self, index):
        step = self.steps[index]
        value = sum(self.terms)
        got = mixed_swap(value, step)
        lower = mixed_bit(step) == 0
        self.terms = [jnp.where(lower, jnp.concatenate([value, got], 0), jnp.concatenate([got, value], 0))]
        return value

    def finish(self):
        mine = self.terms[0].reshape(self.shape)
        return mine, swap(mine, "seq", 1)

    def next(self, *wait):
        if wait:
            self.terms = list(lax.optimization_barrier((*self.terms, *wait))[: len(self.terms)])
        count, place = len(self.steps), self.stage
        self.stage += 1
        if place < count:
            return self.halve(place)
        if place < count + len(self.rests):
            return self.add(self.rests[place - count])
        return self.double(self.last - 1 - place)

    def rest(self):
        while self.stage < self.last:
            self.next()
        return self.finish()


def per_device(
    canvas,
    memory,
    canvas_len,
    memory_len,
    slot_cot,
    self_project,
    self_output,
    self_biases,
    cross_project,
    cross_output,
    cross_biases,
    norm_gains,
    norm_shifts,
    inner_weight,
    inner_bias,
    outer_weight,
    outer_bias,
    slot_weight,
    slot_bias,
):
    block, width = canvas.shape[2:]
    seat = lax.axis_index("seq")
    batch = seat // 2
    upper = batch == 1

    def own_of(value, index):
        return lax.dynamic_index_in_dim(value, index, 0, keepdims=False)

    def placed(kept, got):
        got = got.astype(kept.dtype)
        return jnp.where(upper, jnp.stack([got, kept]), jnp.stack([kept, got]))[:, None]

    kept, away = own_of(canvas, batch)[0], own_of(canvas, 1 - batch)[0]
    scalars = jnp.stack(
        [seat.astype(jnp.int32), own_of(canvas_len, batch)[0], own_of(memory_len, batch)[0]]
    )
    inner_row, outer_row = inner_bias.reshape(1, -1), outer_bias.reshape(1, -1)
    cot_kept, cot_away = own_of(slot_cot, batch)[0], own_of(slot_cot, 1 - batch)[0]
    got, scalars, inner_row, outer_row, cot_away, cot_kept = lax.optimization_barrier(
        (swap(away, "seq", 2), scalars, inner_row, outer_row, cot_away, cot_kept)
    )
    every = [kept, got, swap(kept, "seq", 1), swap(got, "seq", 1)]
    kept, away = own_of(memory, batch)[0], own_of(memory, 1 - batch)[0]
    source_every = [kept, swap(away, "seq", 2), swap(kept, "seq", 1), swap(away, "seq", 3)]
    cots = [cot_kept, swap(cot_away, "seq", 2)]

    q, k, v, p, o, inverse, normal_one, spread_one = attention_forward(
        False, scalars, None, every, self_project, self_biases, self_output, norm_gains, norm_shifts
    )
    low_one, q2, k2, v2, p2, o2, inverse2, normal_two, spread_two = attention_forward(
        True, scalars, normal_one, source_every, cross_project, cross_biases, cross_output, norm_gains, norm_shifts
    )
    cot_halo = jnp.stack([swap(cot_kept[block - 1], "seq", 1), swap(cot_away[block - 1], "seq", 3)])
    feed_keep, feed_send, slot_keep, slot_send, state, grad_two, small_feed = feed_forward(
        scalars, normal_two, norm_gains, norm_shifts, cots, cot_halo, inner_weight, inner_row,
        outer_weight, outer_row, slot_weight,
    )

    feed = Sum(feed_keep, swap(feed_send, "seq", 1), 0)
    state_halo = swap(jnp.stack([state[0], state[block]]), "seq", 1)
    dq2, dk2, dv2, small_cross, grad_mid = attention_backward(
        True, [grad_two, normal_two, spread_two, norm_gains, inverse2, cross_output], o2, q2, k2, v2, p2
    )
    sent = feed.halve(0, [dq2])
    feed.stage = 1
    cross_keep, cross_send, memory_own, memory_other = weight_gradients(
        True, scalars, o2, grad_mid, low_one, source_every, [dq2, dk2, dv2], cross_project,
        slots=[slot_keep, slot_send], later=[sent]
    )
    cross = Sum(cross_keep, swap(cross_send, "seq", 1), 0)
    dq, dk, dv, small_self, grad_first = attention_backward(
        False, [grad_mid, dq2, cross_project, normal_one, spread_one, norm_gains, inverse, self_output],
        o, q, k, v, p, later=[cross_send],
    )
    sent = feed.halve(1)
    feed.stage = 2
    self_keep, self_send, canvas_own, canvas_other = weight_gradients(
        False, scalars, o, grad_first, every[0], every, [dq, dk, dv], self_project,
        slots=[small_feed, small_cross, small_self], later=[sent]
    )
    own = Sum(self_keep, swap(self_send, "seq", 1), 0)

    slots = slot_states(scalars, state, state_halo, slot_weight, slot_bias)
    memory_total = memory_own + swap(memory_other, "seq", 1).astype(F32)
    canvas_total = canvas_own + swap(canvas_other, "seq", 1).astype(F32)

    slots_out = placed(slots[:block], swap(slots[block:], "seq", 2))
    canvas_out = placed(canvas_total[:block], swap(canvas_total[block:].astype(BF16), "seq", 2))
    memory_out = placed(memory_total[:block], swap(memory_total[block:].astype(BF16), "seq", 2))
    c0 = cross.next()
    o0 = own.next()
    c1 = cross.next(o0)
    o1 = own.next(c1)
    f2 = feed.next()
    f3 = feed.next(c1)
    c2 = cross.next(o1)
    o2 = own.next(c2)
    c3 = cross.next(o2)
    feed.next(slots_out)
    cross.next(memory_out)
    own.next()
    own.next(canvas_out)
    (grad_outer, grad_inner, grad_cross_output, grad_cross_project, grad_slot, grad_self_output, grad_self_project,
     grad_self_biases, grad_cross_biases, grad_gains, grad_shifts, grad_inner_bias, grad_outer_bias,
     grad_slot_bias) = finish(scalars, feed.rest(), cross.rest(), own.rest(), inner_bias.shape[0])
    return (
        slots_out,
        canvas_out,
        memory_out,
        grad_self_project,
        grad_self_output,
        grad_self_biases,
        grad_cross_project,
        grad_cross_output,
        grad_cross_biases,
        grad_gains,
        grad_shifts,
        grad_inner,
        grad_inner_bias.reshape(-1),
        grad_outer,
        grad_outer_bias.reshape(-1),
        grad_slot,
        grad_slot_bias.reshape(-1),
    )


def solution(mesh):
    tokens = P(None, "dp", "seq", None)
    sizes = P(None, "dp")
    return jax.shard_map(
        per_device,
        mesh=mesh,
        in_specs=(tokens, tokens, sizes, sizes, tokens) + (P(),) * 14,
        out_specs=(tokens,) * 3 + (P(),) * 14,
        check_vma=False,
    )
```

```python
import functools

import jax
import jax.numpy as jnp
from jax import lax
from jax.experimental import pallas as pl
from jax.experimental.pallas import tpu as pltpu
from jax.sharding import PartitionSpec as P

LANES = 128
CHUNK = 128
BACK_CHUNK = 512
SMALL = 128
EPSILON = 1e-05
MASKED = -1e30
VMEM_LIMIT = 60 << 20
F32 = jnp.float32
BF16 = jnp.bfloat16
BLOCKS = (0, 2, 1, 3)


def product(left, right):
    return jnp.dot(left, right, preferred_element_type=F32)


def left_product(left, right):
    return lax.dot_general(left, right, (((0,), (0,)), ((), ())), preferred_element_type=F32)


def right_product(left, right):
    return lax.dot_general(left, right, (((1,), (1,)), ((), ())), preferred_element_type=F32)


def column_sum(value):
    return jnp.sum(value, 0, keepdims=True)


def norm_forward(value):
    mean = jnp.mean(value, -1, keepdims=True)
    centered = value - mean
    spread = jnp.mean(centered * centered, -1, keepdims=True)
    inverse = lax.rsqrt(spread + EPSILON)
    return centered * inverse, inverse


def norm_backward(upstream, normal, inverse, gain):
    scaled = upstream * gain
    inner_mean = jnp.mean(scaled, -1, keepdims=True)
    cross_mean = jnp.mean(scaled * normal, -1, keepdims=True)
    return inverse * (scaled - inner_mean - normal * cross_mean)


def wide_row(ref, row):
    return ref[row : row + 1, :].astype(F32)


def head_only(value, which):
    lane = lax.broadcasted_iota(jnp.int32, (1, LANES), 1)
    mine = lane < LANES // 2 if which == 0 else lane >= LANES // 2
    return jnp.where(mine, value, jnp.zeros_like(value))


def head_pick(first, second):
    lane = lax.broadcasted_iota(jnp.int32, (1, LANES), 1)
    return jnp.where(lane < LANES // 2, first, second)


def pair_of(step):
    return pl.ds(pl.multiple_of(step * LANES, LANES), LANES)


def forward_body(cross, scalars, *refs):
    if cross:
        rows_in, *refs = refs
    all_in, refs = refs[: len(BLOCKS)], refs[len(BLOCKS) :]
    project, biases, wo, gains, shifts, *refs = refs
    if cross:
        out_low, *refs = refs
    out_q, out_k, out_v, out_p, out_o, out_inverse, out_normal, out_spread = refs[:8]
    every, queries, both_all = refs[8:]
    step = pl.program_id(0)
    block = all_in[0].shape[0]
    width = every.shape[1]
    rows, total = 2 * block, len(BLOCKS) * block
    seat, size = scalars[0], scalars[2 if cross else 1]

    @pl.when(step == 0)
    def _():
        for index, ref in enumerate(all_in):
            every[index * block : (index + 1) * block, :] = ref[...]
        if cross:
            value = rows_in[...] * wide_row(gains, 0) + wide_row(shifts, 0)
            out_low[...] = value.astype(BF16)
            source = out_low[...]
        else:
            source = every[:rows, :]
        query = product(source, project[0]) + wide_row(biases, 0)
        queries[...] = query.astype(BF16) * jnp.asarray(0.125, BF16)
        both_all[0] = product(every[...], project[1]).astype(BF16)
        both_all[1] = (product(every[...], project[2]) + wide_row(biases, 1)).astype(BF16)

    query = queries[:, pair_of(step)]
    keys = both_all[0, :, pair_of(step)]
    values = both_all[1, :, pair_of(step)]
    out_q[...] = query
    out_k[...] = keys
    out_v[...] = values
    wide = jnp.concatenate([values, jnp.ones((total, LANES), BF16)], 1)
    place = lax.broadcasted_iota(jnp.int32, (1, block), 1)
    bias = jnp.concatenate(
        [jnp.where((seat ^ item) * block + place < size, 0.0, MASKED) for item in BLOCKS], 1
    )
    for start in range(0, rows, CHUNK):
        piece = query[start : start + CHUNK]
        parts = []
        for head in range(2):
            scores = right_product(head_only(piece, head), keys) + bias
            weights = jnp.exp(scores - jnp.max(scores, 1, keepdims=True)).astype(BF16)
            out_p[head, start : start + CHUNK, :] = weights
            result = product(weights, wide)
            inverse = 1.0 / result[:, LANES:]
            parts.append((result[:, :LANES] * inverse, inverse))
        out_o[start : start + CHUNK, pair_of(step)] = head_pick(parts[0][0], parts[1][0]).astype(BF16)
        out_inverse[start : start + CHUNK, pair_of(step)] = head_pick(parts[0][1], parts[1][1]).astype(BF16)

    @pl.when(step == pl.num_programs(0) - 1)
    def _():
        if cross:
            base = rows_in[...] * wide_row(gains, 0) + wide_row(shifts, 0)
        else:
            base = every[:rows, :].astype(F32)
        value = base + product(out_o[...], wo[...]) + wide_row(biases, 2)
        normal, inverse = norm_forward(value)
        out_normal[...] = normal
        out_spread[...] = jnp.broadcast_to(inverse, out_spread.shape)


def whole(*shape):
    return pl.BlockSpec(shape, lambda i: (0,) * len(shape))


SMEM = pl.BlockSpec(memory_space=pltpu.SMEM)
LATER = pl.BlockSpec(memory_space=pl.ANY)


def attention_forward(cross, scalars, rows_in, all_in, project, biases, wo, gains, shifts):
    block, width = all_in[0].shape
    rows, total = 2 * block, len(BLOCKS) * block
    pairs = width // LANES
    part = lambda count: pl.BlockSpec((count, LANES), lambda i: (0, i))
    out_shape = [
        jax.ShapeDtypeStruct((rows, width), BF16),
        jax.ShapeDtypeStruct((total, width), BF16),
        jax.ShapeDtypeStruct((total, width), BF16),
        jax.ShapeDtypeStruct((2 * pairs, rows, total), BF16),
        jax.ShapeDtypeStruct((rows, width), BF16),
        jax.ShapeDtypeStruct((rows, width), BF16),
        jax.ShapeDtypeStruct((rows, width), F32),
        jax.ShapeDtypeStruct((rows, LANES), F32),
    ]
    out_specs = [
        part(rows),
        part(total),
        part(total),
        pl.BlockSpec((2, rows, total), lambda i: (i, 0, 0)),
        whole(rows, width),
        whole(rows, width),
        whole(rows, width),
        whole(rows, LANES),
    ]
    if cross:
        out_shape = [jax.ShapeDtypeStruct((rows, width), BF16)] + out_shape
        out_specs = [whole(rows, width)] + out_specs
    return pl.pallas_call(
        functools.partial(forward_body, cross),
        grid=(pairs,),
        in_specs=[SMEM]
        + ([whole(rows, width)] if cross else [])
        + [whole(block, width)] * len(BLOCKS)
        + [whole(3, width, width), whole(3, width), whole(width, width), whole(3, width), whole(3, width)],
        out_specs=out_specs,
        out_shape=out_shape,
        scratch_shapes=[
            pltpu.VMEM((total, width), BF16),
            pltpu.VMEM((rows, width), BF16),
            pltpu.VMEM((2, total, width), BF16),
        ],
        compiler_params=pltpu.CompilerParams(vmem_limit_bytes=VMEM_LIMIT),
        cost_estimate=pl.CostEstimate(
            flops=2 * rows * total * width * 8, bytes_accessed=20 << 20, transcendentals=rows * total * 8
        ),
        name="cross_forward" if cross else "self_forward",
    )(scalars, *([rows_in] if cross else []), *all_in, project, biases, wo, gains, shifts)


def backward_body(cross, *refs):
    if cross:
        upstream_in, *refs = refs
    else:
        base_in, query_two, wq, *refs = refs
    normal, spread, gains, inverse, wo, mixed, query, keys, values, weights = refs[:10]
    out_query, out_key, out_value, out_small, out_rows, mixed_grad = refs[-6:]
    step = pl.program_id(0)
    rows, width = mixed.shape
    total = keys.shape[0]
    pair = pair_of(step)

    @pl.when(step == 0)
    def _():
        out_small[...] = jnp.zeros(out_small.shape, F32)
        if cross:
            upstream = upstream_in[...]
        else:
            upstream = base_in[...] + right_product(query_two[...], wq[0])
        normal_now = normal[...]
        grad = norm_backward(upstream, normal_now, spread[:, 0:1], wide_row(gains, 1 if cross else 0))
        out_small[0:1, :] = column_sum(upstream * normal_now)
        out_small[1:2, :] = column_sum(upstream)
        out_small[2:3, :] = column_sum(grad)
        out_rows[...] = grad
        mixed_grad[...] = (right_product(grad.astype(BF16), wo[...]) * inverse[...].astype(F32)).astype(BF16)

    keys_now, values_now = keys[...], values[...]
    key_grad = jnp.zeros((LANES, total), F32)
    value_grad = jnp.zeros((LANES, total), F32)
    query_grads = []
    for start in range(0, rows, BACK_CHUNK):
        span = slice(start, start + BACK_CHUNK)
        piece = query[span, :]
        grad = mixed_grad[span, pair]
        center = grad.astype(F32) * mixed[span, pair].astype(F32)
        found = []
        for head in range(2):
            grad_now = head_only(grad, head)
            center_now = jnp.sum(head_only(center, head), 1, keepdims=True)
            weight = weights[head, span, :]
            slope = right_product(grad_now, values_now)
            score_grad = (weight.astype(F32) * (slope - center_now)).astype(BF16)
            found.append(product(score_grad, keys_now))
            value_grad = value_grad + left_product(grad_now, weight)
            key_grad = key_grad + left_product(head_only(piece, head), score_grad)
        query_grads.append(head_pick(found[0], found[1]) * 0.125)
    query_grad = jnp.concatenate(query_grads, 0)
    value_grad = value_grad.T
    out_small[3:4, pair] = column_sum(query_grad)
    out_small[4:5, pair] = column_sum(value_grad)
    out_query[...] = query_grad.astype(BF16)
    out_key[...] = key_grad.T.astype(BF16)
    out_value[...] = value_grad.astype(BF16)


def attention_backward(cross, first_inputs, mixed, query, keys, values, weights, later=()):
    rows, width = mixed.shape
    total = keys.shape[0]
    pairs = width // LANES
    part = lambda count: pl.BlockSpec((count, LANES), lambda i: (0, i))
    front = [whole(1, *value.shape[1:]) if value.ndim == 3 else whole(*value.shape) for value in first_inputs]
    return pl.pallas_call(
        functools.partial(backward_body, cross),
        grid=(pairs,),
        in_specs=front
        + [whole(rows, width), part(rows), part(total), part(total)]
        + [pl.BlockSpec((2, rows, total), lambda i: (i, 0, 0))]
        + [LATER] * len(later),
        out_specs=[part(rows), part(total), part(total), whole(8, width), whole(rows, width)],
        out_shape=[
            jax.ShapeDtypeStruct((rows, width), BF16),
            jax.ShapeDtypeStruct((total, width), BF16),
            jax.ShapeDtypeStruct((total, width), BF16),
            jax.ShapeDtypeStruct((8, width), F32),
            jax.ShapeDtypeStruct((rows, width), F32),
        ],
        scratch_shapes=[pltpu.VMEM((rows, width), BF16)],
        compiler_params=pltpu.CompilerParams(vmem_limit_bytes=VMEM_LIMIT),
        cost_estimate=pl.CostEstimate(
            flops=2 * rows * total * width * 16, bytes_accessed=20 << 20, transcendentals=0
        ),
        name="cross_backward" if cross else "self_backward",
    )(*first_inputs, mixed, query, keys, values, weights, *later)


def weights_body(cross, scalars, *refs):
    ins, refs = refs[:11], refs[11:]
    if cross:
        slots, refs = refs[:2], refs[2:]
    else:
        smalls, refs = refs[:3], refs[3:]
    refs = refs[-18:]
    out_keep, out_send, out_own, out_other = refs[:4]
    mixed, grad_in, rows_in, every, query_in, key_in, value_in, project, grads, own, other, sem_in, sem_out = refs[4:17]
    rows, width = mixed.shape
    block = rows // 2
    even = lax.rem(scalars[0], 2) == 0
    here = [mixed, grad_in, rows_in, *[every.at[pl.ds(i * block, block)] for i in range(len(BLOCKS))],
            query_in, key_in, value_in, project]
    wanted = [0, 1, 2, 7, 3, 4, 5, 6, 8, 9, 10] if cross else [0, 1, 3, 4, 7, 5, 6, 8, 9, 10]
    coming = {i: pltpu.make_async_copy(ins[i], here[i], sem_in.at[i]) for i in wanted}
    for i in wanted:
        coming[i].start()

    def arrive(*which):
        for i in which:
            coming[i].wait()

    def span(index, count):
        return pl.ds(index * width, count)

    def leave(kept_by_even, index, value, number):
        count = value.shape[0]

        @pl.when(even if kept_by_even else jnp.logical_not(even))
        def _():
            pltpu.make_async_copy(value, out_keep.at[span(index, count)], sem_out.at[number]).start()

        @pl.when(jnp.logical_not(even) if kept_by_even else even)
        def _():
            pltpu.make_async_copy(value, out_send.at[span(index, count)], sem_out.at[number]).start()

    going = [pltpu.make_async_copy(grads.at[i], out_keep.at[span(i % 2, width)], sem_out.at[i]) for i in range(4)]
    if cross:
        extra = refs[17]
        slot_in = [pltpu.make_async_copy(slots[i], extra.at[i], sem_in.at[11 + i]) for i in range(2)]
        for i, out in enumerate((out_keep, out_send)):
            going.append(pltpu.make_async_copy(extra.at[i], out.at[span(2, width)], sem_out.at[4 + i]))
            slot_in[i].start()
    else:
        extra = refs[17]
        extra[0] = jnp.concatenate([ref[...] for ref in smalls] + [jnp.zeros((SMALL - 24, width), F32)], 0).astype(BF16)
        extra[1] = jnp.zeros((SMALL, width), BF16)
        for i in range(2):
            going.append(pltpu.make_async_copy(extra.at[i], out_keep.at[span(2, SMALL)], sem_out.at[4 + i]))
            leave(i == 0, 2, extra.at[i], 4 + i)

    arrive(0, 1)
    grads[0] = left_product(mixed[...], grad_in[...].astype(BF16)).astype(BF16)
    leave(True, 0, grads.at[0], 0)
    if cross:
        for i in range(2):
            slot_in[i].wait()
            going[4 + i].start()
        arrive(2, 7)
        grads[1] = left_product(rows_in[...], query_in[...]).astype(BF16)
    else:
        arrive(3, 4, 7)
        grads[1] = left_product(every[:rows, :], query_in[...]).astype(BF16)
    leave(True, 1, grads.at[1], 1)
    if cross:
        arrive(3, 4, 5, 6, 8)
    else:
        arrive(5, 6, 8)
    grads[2] = left_product(every[...], key_in[...]).astype(BF16)
    leave(False, 0, grads.at[2], 2)
    arrive(9)
    grads[3] = left_product(every[...], value_in[...]).astype(BF16)
    leave(False, 1, grads.at[3], 3)
    arrive(10)

    def onward(part):
        return right_product(key_in[part, :], project[1]) + right_product(value_in[part, :], project[2])

    other[...] = onward(slice(rows, 2 * rows)).astype(BF16)
    going.append(pltpu.make_async_copy(other, out_other, sem_out.at[6]))
    going[-1].start()
    value = onward(slice(0, rows))
    if not cross:
        value = value + grad_in[...] + right_product(query_in[...], project[0])
    own[...] = value
    going.append(pltpu.make_async_copy(own, out_own, sem_out.at[7]))
    going[-1].start()
    for copy in going:
        copy.wait()


VMEM = pl.BlockSpec(memory_space=pltpu.VMEM)


def weight_gradients(cross, scalars, mixed, grad, rows_in, all_in, grads, project, slots=(), later=()):
    block, width = all_in[0].shape
    rows, total = 2 * block, len(BLOCKS) * block
    count = 3 * width if cross else 2 * width + SMALL
    scratch = [
        pltpu.VMEM((rows, width), BF16),
        pltpu.VMEM((rows, width), F32),
        pltpu.VMEM((rows, width), BF16),
        pltpu.VMEM((total, width), BF16),
        pltpu.VMEM((rows, width), BF16),
        pltpu.VMEM((total, width), BF16),
        pltpu.VMEM((total, width), BF16),
        pltpu.VMEM((3, width, width), BF16),
        pltpu.VMEM((4, width, width), BF16),
        pltpu.VMEM((rows, width), F32),
        pltpu.VMEM((total - rows, width), BF16),
        pltpu.SemaphoreType.DMA((13,)),
        pltpu.SemaphoreType.DMA((8,)),
    ]
    scratch.append(pltpu.VMEM((2, width if cross else SMALL, width), BF16))
    return pl.pallas_call(
        functools.partial(weights_body, cross),
        in_specs=[SMEM] + [LATER] * 11 + [LATER if cross else VMEM] * len(slots) + [LATER] * len(later),
        out_specs=[LATER] * 4,
        out_shape=[
            jax.ShapeDtypeStruct((count, width), BF16),
            jax.ShapeDtypeStruct((count, width), BF16),
            jax.ShapeDtypeStruct((rows, width), F32),
            jax.ShapeDtypeStruct((total - rows, width), BF16),
        ],
        scratch_shapes=scratch,
        compiler_params=pltpu.CompilerParams(vmem_limit_bytes=VMEM_LIMIT),
        cost_estimate=pl.CostEstimate(flops=24 * rows * width * width, bytes_accessed=12 << 20, transcendentals=0),
        name="cross_weights" if cross else "self_weights",
    )(scalars, mixed, grad, rows_in, *all_in, *grads, project, *slots, *later)


SPLIT = 2


def gelu(value):
    square = value * value
    bent = jnp.tanh(0.7978845608028654 * value * (1.0 + 0.044715 * square))
    half = 0.5 * (1.0 + bent)
    slope = half + 0.5 * value * (1.0 - bent * bent) * (0.7978845608028654 + 3 * 0.044715 * 0.7978845608028654 * square)
    return value * half, slope


def feed_body(scalars, normal_two, gains, shifts, cot_one, cot_two, halo, wi, bi, wo, bo, slot_weight,
              out_keep, out_send, out_slot_keep, out_slot_send, out_state, out_grad, out_small,
              low, slopes, active, acc, low_grad):
    step = pl.program_id(0)
    rows, width = normal_two.shape
    block = rows // 2
    span = wi.shape[1]
    seat, size = scalars[0], scalars[1]
    even = lax.rem(seat, 2) == 0

    def store(kept_by_even, keep, send, index, value):
        value = value.astype(BF16)

        @pl.when(even if kept_by_even else jnp.logical_not(even))
        def _():
            keep[index] = value

        @pl.when(jnp.logical_not(even) if kept_by_even else even)
        def _():
            send[index] = value

    @pl.when(step == 0)
    def _():
        value = normal_two[...] * wide_row(gains, 1) + wide_row(shifts, 1)
        low[...] = value.astype(BF16)
        acc[...] = value + bo[...].astype(F32)

    @pl.when(step < SPLIT)
    def _():
        start = step * span
        value = product(low[...], wi[...]) + bi[...].astype(F32)
        found, slope = gelu(value)
        place = pl.ds(pl.multiple_of(start, span), span)
        slopes[:, place] = slope
        active[:, place] = found.astype(BF16)
        acc[...] += product(active[:, place], wo[...])

    @pl.when(step == SPLIT)
    def _():
        normal, inverse = norm_forward(acc[...])
        state = (normal * wide_row(gains, 2) + wide_row(shifts, 2)).astype(BF16)
        out_state[...] = state
        out_small[...] = jnp.zeros(out_small.shape, F32)
        place = lax.broadcasted_iota(jnp.int32, (block, 1), 0)
        sides = []
        for index, (item, cot) in enumerate(zip(BLOCKS[:2], (cot_one, cot_two))):
            first = (seat ^ item) * block
            value = cot[...].astype(F32)
            straight = jnp.where(first + place + 1 < size, value, 0.0)
            before = jnp.where(even, wide_row(halo, 1 - index), wide_row(halo, index))
            moved = jnp.where(place == 0, before, pltpu.roll(value, 1, 0))
            moved = jnp.where((first + place < size) & (first + place > 0), moved, 0.0)
            sides.append(jnp.concatenate([straight, moved], 1))
        sides = jnp.concatenate(sides, 0)
        out_small[0:1, :] = column_sum(sides[:, :width])
        sides = sides.astype(BF16)
        slot_grad = left_product(state, sides)
        store(True, out_slot_keep, out_slot_send, slice(None), slot_grad[:, :width])
        store(False, out_slot_keep, out_slot_send, slice(None), slot_grad[:, width:])
        state_grad = right_product(
            sides, jnp.concatenate([slot_weight[:width, :], slot_weight[width:, :]], 1)
        )
        out_small[1:2, :] = column_sum(state_grad * normal)
        out_small[2:3, :] = column_sum(state_grad)
        grad = norm_backward(state_grad, normal, inverse, wide_row(gains, 2))
        out_small[3:4, :] = column_sum(grad)
        acc[...] = grad
        low_grad[...] = grad.astype(BF16)

    @pl.when(step > SPLIT)
    def _():
        start = (step - SPLIT - 1) * span
        place = pl.ds(pl.multiple_of(start, span), span)
        grad = right_product(low_grad[...], wo[...]) * slopes[:, place]
        sums = column_sum(grad)
        first = 4 + (step - SPLIT - 1) * (span // width)
        for part in range(0, span, width):
            out_small[pl.ds(first + part // width, 1), :] = sums[:, part : part + width]
        grad_low = grad.astype(BF16)
        outer = left_product(active[:, place], low_grad[...])
        inner = left_product(low[...], grad_low)
        for part in range(0, span, width):
            store(True, out_keep, out_send, part // width, outer[part : part + width, :])
            store(False, out_keep, out_send, part // width, inner[:, part : part + width])
        acc[...] += right_product(grad_low, wi[...])

    @pl.when(step == pl.num_programs(0) - 1)
    def _():
        out_grad[...] = acc[...]


def feed_forward(scalars, normal_two, gains, shifts, cots, halo, wi, bi, wo, bo, slot_weight):
    rows, width = normal_two.shape
    hidden = wi.shape[1]
    span = hidden // SPLIT
    part = lambda i: jnp.where(i < SPLIT, i, jnp.maximum(i - SPLIT - 1, 0))
    group = pl.BlockSpec((span // width, width, width), lambda i: (jnp.maximum(i - SPLIT - 1, 0), 0, 0))
    grads = jax.ShapeDtypeStruct((hidden // width, width, width), BF16)
    slot = jax.ShapeDtypeStruct((width, width), BF16)
    return pl.pallas_call(
        feed_body,
        grid=(2 * SPLIT + 1,),
        in_specs=[
            SMEM,
            whole(rows, width),
            whole(3, width),
            whole(3, width),
            whole(rows // 2, width),
            whole(rows // 2, width),
            whole(2, width),
            pl.BlockSpec((width, span), lambda i: (0, part(i))),
            pl.BlockSpec((1, span), lambda i: (0, part(i))),
            pl.BlockSpec((span, width), lambda i: (part(i), 0)),
            whole(1, width),
            whole(2 * width, width),
        ],
        out_specs=[group, group, whole(width, width), whole(width, width), whole(rows, width), whole(rows, width),
                   whole(8, width)],
        out_shape=[
            grads,
            grads,
            slot,
            slot,
            jax.ShapeDtypeStruct((rows, width), BF16),
            jax.ShapeDtypeStruct((rows, width), F32),
            jax.ShapeDtypeStruct((8, width), F32),
        ],
        scratch_shapes=[
            pltpu.VMEM((rows, width), BF16),
            pltpu.VMEM((rows, hidden), F32),
            pltpu.VMEM((rows, hidden), BF16),
            pltpu.VMEM((rows, width), F32),
            pltpu.VMEM((rows, width), BF16),
        ],
        compiler_params=pltpu.CompilerParams(vmem_limit_bytes=VMEM_LIMIT),
        cost_estimate=pl.CostEstimate(
            flops=2 * rows * width * width * 32, bytes_accessed=20 << 20, transcendentals=rows * width * 8
        ),
        name="feed_forward",
    )(scalars, normal_two, gains, shifts, *cots, halo, wi, bi, wo, bo, slot_weight)


def slot_body(scalars, state, halo, slot_weight, slot_bias, out):
    rows, width = state.shape
    block = rows // 2
    seat, size = scalars[0], scalars[1]
    even = lax.rem(seat, 2) == 0
    place = lax.broadcasted_iota(jnp.int32, (block, 1), 0)
    for index, item in enumerate(BLOCKS[:2]):
        span = slice(index * block, (index + 1) * block)
        value = state[span, :]
        after = jnp.where(even, wide_row(halo, index), wide_row(halo, 1 - index))
        moved = jnp.where(place == block - 1, after, pltpu.roll(value.astype(F32), block - 1, 0)).astype(BF16)
        result = product(value, slot_weight[:width, :]) + product(moved, slot_weight[width:, :])
        result = result + slot_bias[...].astype(F32)
        out[span, :] = jnp.where((seat ^ item) * block + place + 1 < size, result, 0.0).astype(BF16)


def slot_states(scalars, state, halo, slot_weight, slot_bias):
    rows, width = state.shape
    vmem = pl.BlockSpec(memory_space=pltpu.VMEM)
    return pl.pallas_call(
        slot_body,
        in_specs=[SMEM] + [vmem] * 4,
        out_specs=vmem,
        out_shape=jax.ShapeDtypeStruct((rows, width), BF16),
        compiler_params=pltpu.CompilerParams(vmem_limit_bytes=16 << 20),
        cost_estimate=pl.CostEstimate(flops=4 * rows * width * width, bytes_accessed=4 << 20, transcendentals=0),
        name="slot_states",
    )(scalars, state, halo, slot_weight, slot_bias.reshape(1, -1))


def finish_body(hidden_parts, scalars, *refs):
    halves, refs = refs[:6], refs[6:]
    (out_outer, out_inner, out_cross_output, out_cross_project, out_slot, out_self_output, out_self_project,
     out_self, out_cross, out_gain, out_shift, out_inner_bias, out_outer_bias, out_slot_bias,
     feed, cross, own, wide, sem_in, sem_out) = refs
    width = feed.shape[2]
    odd = lax.rem(scalars[0], 2)
    groups = (feed, cross, own)
    coming = [
        [pltpu.make_async_copy(halves[2 * i + j], group.at[j], sem_in.at[2 * i + j]) for j in range(2)]
        for i, group in enumerate(groups)
    ]
    for pair in coming:
        for copy in pair:
            copy.start()
    rows = lambda index: pl.ds(index * width, width)
    targets = [
        [(i, 0, out_outer.at[rows(i)]) for i in range(hidden_parts)]
        + [(i, 1, out_inner.at[:, rows(i)]) for i in range(hidden_parts)],
        [(0, 0, out_cross_output), (1, 0, out_cross_project.at[0]), (2, 0, out_slot.at[rows(0)]),
         (0, 1, out_cross_project.at[1]), (1, 1, out_cross_project.at[2]), (2, 1, out_slot.at[rows(1)])],
        [(0, 0, out_self_output), (1, 0, out_self_project.at[0]),
         (0, 1, out_self_project.at[1]), (1, 1, out_self_project.at[2])],
    ]
    going = []
    for pair, group, places in zip(coming, groups, targets):
        for copy in pair:
            copy.wait()
        for chunk, side, out in places:
            number = len(going)
            source = odd if side == 0 else 1 - odd
            wide[number] = group[source, rows(chunk), :].astype(F32)
            going.append(pltpu.make_async_copy(wide.at[number], out, sem_out.at[number]))
            going[-1].start()
    small = own[odd, pl.ds(2 * width, 32), :].astype(F32)
    pick = lambda *places: jnp.concatenate([small[place : place + 1, :] for place in places], 0)
    out_self[...] = pick(19, 20, 18)
    out_cross[...] = pick(11, 12, 10)
    out_gain[...] = pick(16, 8, 1)
    out_shift[...] = pick(17, 9, 2)
    out_inner_bias[...] = jnp.concatenate([small[4 + i : 5 + i, :] for i in range(hidden_parts)], 1)
    out_outer_bias[...] = pick(3)
    out_slot_bias[...] = pick(0)
    for copy in going:
        copy.wait()


def finish(scalars, feed, cross, own, hidden):
    width = feed[0].shape[-1]
    parts = hidden // width
    feed = [value.reshape(-1, width) for value in feed]
    count = 2 * parts + 10
    shape = lambda *dims: jax.ShapeDtypeStruct(dims, F32)
    return pl.pallas_call(
        functools.partial(finish_body, parts),
        in_specs=[SMEM] + [LATER] * 6,
        out_specs=[LATER] * 7 + [VMEM] * 7,
        out_shape=[
            shape(hidden, width),
            shape(width, hidden),
            shape(width, width),
            shape(3, width, width),
            shape(2 * width, width),
            shape(width, width),
            shape(3, width, width),
            *[shape(3, width)] * 4,
            shape(1, hidden),
            shape(1, width),
            shape(1, width),
        ],
        scratch_shapes=[pltpu.VMEM((2, *value[0].shape), BF16) for value in (feed, cross, own)]
        + [pltpu.VMEM((count, width, width), F32), pltpu.SemaphoreType.DMA((6,)), pltpu.SemaphoreType.DMA((count,))],
        compiler_params=pltpu.CompilerParams(vmem_limit_bytes=VMEM_LIMIT),
        cost_estimate=pl.CostEstimate(flops=0, bytes_accessed=28 << 20, transcendentals=0),
        name="finish",
    )(scalars, *feed, *cross, *own)


def gate(values, after):
    count = len(values)
    return pl.pallas_call(
        lambda *refs: None,
        in_specs=[LATER] * (count + len(after)),
        out_specs=[LATER] * count,
        out_shape=[jax.ShapeDtypeStruct(value.shape, value.dtype) for value in values],
        input_output_aliases={index: index for index in range(count)},
        name="gate",
    )(*values, *after)


def swap(value, axis, bit):
    count = lax.axis_size(axis)
    return lax.ppermute(value, axis, [(place, place ^ bit) for place in range(count)])


def bit_of(axis, bit):
    return (lax.axis_index(axis) // bit) % 2


def routes():
    across, along = ("dp", 1), ("seq", 2)
    return [(across, along), (along, across)]


def rest_of_dp():
    rest, bit = [], 2
    while bit < lax.axis_size("dp"):
        rest.append(("dp", bit))
        bit *= 2
    return rest


def mixed_swap(value, step):
    if step[0] == step[1]:
        return swap(value, *step[0])
    groups, seats = lax.axis_size("dp"), lax.axis_size("seq")
    pairs = []
    for group in range(groups):
        for seat in range(seats):
            axis, bit = step[seat % 2]
            target = (group ^ bit, seat) if axis == "dp" else (group, seat ^ bit)
            pairs.append((group * seats + seat, target[0] * seats + target[1]))
    return lax.ppermute(value, ("dp", "seq"), pairs)


def mixed_bit(step):
    if step[0] == step[1]:
        return bit_of(*step[0])
    return jnp.where(lax.axis_index("seq") % 2 == 0, bit_of(*step[0]), bit_of(*step[1]))


class Sum:
    def __init__(self, keep, got, depth):
        self.shape = keep.shape
        self.terms = [keep.reshape(-1, keep.shape[-1]), got.reshape(-1, keep.shape[-1])]
        rest = rest_of_dp()
        self.steps = routes() + [(step, step) for step in rest[:depth]]
        self.rests = rest[depth:]
        self.stage = 0
        self.last = 2 * len(self.steps) + len(self.rests)

    def halve(self, index, after=()):
        step = self.steps[index]
        half = self.terms[0].shape[0] // 2
        mine = mixed_bit(step) * half
        cut = lambda start: sum(lax.dynamic_slice_in_dim(term, start, half, 0) for term in self.terms)
        sent = cut(half - mine)
        if after:
            (sent,) = gate([sent], after)
        self.terms = [cut(mine), mixed_swap(sent, step)]
        return sent

    def add(self, step):
        value = sum(self.terms)
        self.terms = [value, swap(value, *step)]
        return value

    def double(self, index):
        step = self.steps[index]
        value = sum(self.terms)
        got = mixed_swap(value, step)
        lower = mixed_bit(step) == 0
        self.terms = [jnp.where(lower, jnp.concatenate([value, got], 0), jnp.concatenate([got, value], 0))]
        return value

    def finish(self):
        mine = self.terms[0].reshape(self.shape)
        return mine, swap(mine, "seq", 1)

    def next(self, *wait):
        if wait:
            self.terms = list(lax.optimization_barrier((*self.terms, *wait))[: len(self.terms)])
        count, place = len(self.steps), self.stage
        self.stage += 1
        if place < count:
            return self.halve(place)
        if place < count + len(self.rests):
            return self.add(self.rests[place - count])
        return self.double(self.last - 1 - place)

    def rest(self):
        while self.stage < self.last:
            self.next()
        return self.finish()


def per_device(
    canvas,
    memory,
    canvas_len,
    memory_len,
    slot_cot,
    self_project,
    self_output,
    self_biases,
    cross_project,
    cross_output,
    cross_biases,
    norm_gains,
    norm_shifts,
    inner_weight,
    inner_bias,
    outer_weight,
    outer_bias,
    slot_weight,
    slot_bias,
):
    block, width = canvas.shape[2:]
    seat = lax.axis_index("seq")
    batch = seat // 2
    upper = batch == 1

    def own_of(value, index):
        return lax.dynamic_index_in_dim(value, index, 0, keepdims=False)

    def placed(kept, got):
        got = got.astype(kept.dtype)
        return jnp.where(upper, jnp.stack([got, kept]), jnp.stack([kept, got]))[:, None]

    kept, away = own_of(canvas, batch)[0], own_of(canvas, 1 - batch)[0]
    scalars = jnp.stack(
        [seat.astype(jnp.int32), own_of(canvas_len, batch)[0], own_of(memory_len, batch)[0]]
    )
    inner_row, outer_row = inner_bias.reshape(1, -1), outer_bias.reshape(1, -1)
    cot_kept, cot_away = own_of(slot_cot, batch)[0], own_of(slot_cot, 1 - batch)[0]
    got, scalars, inner_row, outer_row, cot_away, cot_kept = lax.optimization_barrier(
        (swap(away, "seq", 2), scalars, inner_row, outer_row, cot_away, cot_kept)
    )
    every = [kept, got, swap(kept, "seq", 1), swap(got, "seq", 1)]
    kept, away = own_of(memory, batch)[0], own_of(memory, 1 - batch)[0]
    source_every = [kept, swap(away, "seq", 2), swap(kept, "seq", 1), swap(away, "seq", 3)]
    cots = [cot_kept, swap(cot_away, "seq", 2)]

    q, k, v, p, o, inverse, normal_one, spread_one = attention_forward(
        False, scalars, None, every, self_project, self_biases, self_output, norm_gains, norm_shifts
    )
    low_one, q2, k2, v2, p2, o2, inverse2, normal_two, spread_two = attention_forward(
        True, scalars, normal_one, source_every, cross_project, cross_biases, cross_output, norm_gains, norm_shifts
    )
    cot_halo = jnp.stack([swap(cot_kept[block - 1], "seq", 1), swap(cot_away[block - 1], "seq", 3)])
    feed_keep, feed_send, slot_keep, slot_send, state, grad_two, small_feed = feed_forward(
        scalars, normal_two, norm_gains, norm_shifts, cots, cot_halo, inner_weight, inner_row,
        outer_weight, outer_row, slot_weight,
    )

    feed = Sum(feed_keep, swap(feed_send, "seq", 1), 0)
    state_halo = swap(jnp.stack([state[0], state[block]]), "seq", 1)
    dq2, dk2, dv2, small_cross, grad_mid = attention_backward(
        True, [grad_two, normal_two, spread_two, norm_gains, inverse2, cross_output], o2, q2, k2, v2, p2
    )
    sent = feed.halve(0, [dq2])
    feed.stage = 1
    cross_keep, cross_send, memory_own, memory_other = weight_gradients(
        True, scalars, o2, grad_mid, low_one, source_every, [dq2, dk2, dv2], cross_project,
        slots=[slot_keep, slot_send], later=[sent]
    )
    cross = Sum(cross_keep, swap(cross_send, "seq", 1), 0)
    dq, dk, dv, small_self, grad_first = attention_backward(
        False, [grad_mid, dq2, cross_project, normal_one, spread_one, norm_gains, inverse, self_output],
        o, q, k, v, p, later=[cross_send],
    )
    sent = feed.halve(1, [dq])
    feed.stage = 2
    self_keep, self_send, canvas_own, canvas_other = weight_gradients(
        False, scalars, o, grad_first, every[0], every, [dq, dk, dv], self_project,
        slots=[small_feed, small_cross, small_self], later=[sent]
    )
    own = Sum(self_keep, swap(self_send, "seq", 1), 0)

    slots = slot_states(scalars, state, state_halo, slot_weight, slot_bias)
    memory_total = memory_own + swap(memory_other, "seq", 1).astype(F32)
    canvas_total = canvas_own + swap(canvas_other, "seq", 1).astype(F32)

    slots_out = placed(slots[:block], swap(slots[block:], "seq", 2))
    canvas_out = placed(canvas_total[:block], swap(canvas_total[block:].astype(BF16), "seq", 2))
    memory_out = placed(memory_total[:block], swap(memory_total[block:].astype(BF16), "seq", 2))
    c0 = cross.next()
    o0 = own.next()
    c1 = cross.next(o0)
    o1 = own.next(c1)
    f2 = feed.next()
    f3 = feed.next(c1)
    c2 = cross.next(o1)
    o2 = own.next(c2)
    c3 = cross.next(o2)
    feed.next(slots_out)
    cross.next(memory_out)
    own.next()
    own.next(canvas_out)
    (grad_outer, grad_inner, grad_cross_output, grad_cross_project, grad_slot, grad_self_output, grad_self_project,
     grad_self_biases, grad_cross_biases, grad_gains, grad_shifts, grad_inner_bias, grad_outer_bias,
     grad_slot_bias) = finish(scalars, feed.rest(), cross.rest(), own.rest(), inner_bias.shape[0])
    return (
        slots_out,
        canvas_out,
        memory_out,
        grad_self_project,
        grad_self_output,
        grad_self_biases,
        grad_cross_project,
        grad_cross_output,
        grad_cross_biases,
        grad_gains,
        grad_shifts,
        grad_inner,
        grad_inner_bias.reshape(-1),
        grad_outer,
        grad_outer_bias.reshape(-1),
        grad_slot,
        grad_slot_bias.reshape(-1),
    )


def solution(mesh):
    tokens = P(None, "dp", "seq", None)
    sizes = P(None, "dp")
    return jax.shard_map(
        per_device,
        mesh=mesh,
        in_specs=(tokens, tokens, sizes, sizes, tokens) + (P(),) * 14,
        out_specs=(tokens,) * 3 + (P(),) * 14,
        check_vma=False,
    )
```
